32 devices in a mesh: groups: 2 (over y), seq: 4 (over z), section: 4 (over x, core).
Axes of the slice: x: 2, y: 2, z: 4, core: 2. Of those that a mesh axis runs over, the one named last changes fastest.
Arguments:
- hidden: bfloat16 [4, 32, 3072], P('section', ('groups', 'seq')), parts along dimension 1, may hold values from -6 to 6
- kv_cache: bfloat16 [4, 4, 32, 2, 3072], P('section', None, ('groups', 'seq')), parts along dimension 2, may hold values from -400 to 400
- w_qkv: bfloat16 [4, 3072, 3, 3072], P('section', None, None, 'seq'), may hold values from -0.109375 to 0.109375
- w_out: bfloat16 [4, 3072, 3072], P('section', None, 'seq'), may hold values from -0.109375 to 0.109375
- norm_gain: float32 [4, 2, 128], P('section'), may hold values from 1 to 2
- modulation: float32 [4, 4, 3, 3072], P('section'), may hold values from -5 to 5
- patch_order: int32 [8], P('groups'), parts along dimension 0, may hold values from 0 to 3, each once
- timestep: int32 [8], P('groups'), parts along dimension 0, may hold values from 0 to 3
Outputs:
- next_hidden: bfloat16 [4, 32, 3072], P('section', ('groups', 'seq')), parts along dimension 1
- fresh_kv: bfloat16 [4, 32, 2, 3072], P('section', ('groups', 'seq')), parts along dimension 1
The draws below stay inside these ranges and needn't reach their ends.
There are 2 independent parts, one for each index of `groups`. The reference program is written for one: setup_inputs(seed, part) draws one part's arguments, and reference() takes and returns one part's arrays. A program takes and returns all parts, laid end to end along the dimension named above; an argument that names none is the same for every part. Nothing has to cross between parts.
Inputs may be any that keep to these rules, and one draw needn't show every extreme that they name: `patch_order`: each section holds a different patch.
All inputs are finite; a program needn't handle non-finite values.
Results may differ from the reference program's by a relative error of at most 0.02.
The reference program's roundings to bfloat16 on the way count: a program that leaves them out, or rounds other values in their place, can miss the bound.
Values may be sent and summed in bfloat16 or wider, within the bound.
A program may use at most 64 MiB of HBM per device.

```python
import math
import jax
import jax.numpy as jnp
from jax import lax

D = 3072
HEADS = 24
HEAD = 128
STEPS = 4
TOK_DEV = 4
PATCHES = 4
T_PATCH = 16
LENGTH = 64
N_SECTION = 4


def draw_kv_cache(key, part):
    key_a, key_b = jax.random.split(jax.random.fold_in(key, 11), 2)
    shape = (N_SECTION, PATCHES, T_PATCH, HEADS, HEAD)
    key_part = 1.5 * jax.random.normal(key_a, shape, jnp.float32)
    value_part = jax.random.normal(key_b, shape, jnp.float32)
    key_part = jnp.clip(key_part, -400.0, 400.0)
    stacked = jnp.stack([key_part.reshape(N_SECTION, PATCHES, T_PATCH, D), value_part.reshape(N_SECTION, PATCHES, T_PATCH, D)], axis=3)
    return stacked.astype(jnp.bfloat16)


def plant(array, key, smallest, top_value):
    place = [jax.random.randint(jax.random.fold_in(key, axis), (), 0, length) for axis, length in enumerate(array.shape)]
    widest = array.shape.index(max(array.shape))
    next_to = place[:widest] + [(place[widest] + 1) % array.shape[widest]] + place[widest + 1:]
    return array.at[tuple(place)].set(smallest).at[tuple(next_to)].set(top_value)


def levels(key, shape, pieces, smallest, high):
    level = 1.0
    for dim, blocks in pieces:
        draws = jax.random.uniform(jax.random.fold_in(jax.random.fold_in(key, 6), dim), (blocks,), jnp.float32, smallest / len(pieces), high / len(pieces))
        level = level * jnp.repeat(jnp.exp(draws), shape[dim] // blocks).reshape((-1,) + (1,) * (len(shape) - 1 - dim))
    return level


def gaussian(rng, extent, scale, bound, cuts=(), held_as=jnp.bfloat16):
    drawn = scale * jax.random.normal(rng, extent, jnp.float32)
    if cuts:
        drawn = drawn * levels(rng, extent, cuts, -0.22, 0.18)
    return jnp.clip(drawn, -bound, bound).astype(held_as)


def setup_inputs(seed: int = 0, part: int = 0) -> dict:
    seeds = jax.random.split(jax.random.key(seed), 9)
    part_splits = jax.random.split(jax.random.fold_in(seeds[8], part), 9)
    return {
        "hidden": gaussian(part_splits[0], (N_SECTION, T_PATCH, D), 1.0, 6.0, ((0, 4), (1, 4))),
        "kv_cache": draw_kv_cache(jax.random.fold_in(jax.random.fold_in(seeds[8], part), 71), part),
        "w_qkv": gaussian(seeds[2], (N_SECTION, D, 3, D), D ** -0.5, 0.109375, ((0, 4), (3, 4))),
        "w_out": gaussian(seeds[3], (N_SECTION, D, D), D ** -0.5, 0.109375, ((0, 4), (2, 4))),
        "norm_gain": jnp.clip(1.0 + 1.0 * jax.random.uniform(seeds[4], (N_SECTION, 2, HEAD), jnp.float32) ** levels(seeds[4], (N_SECTION, 2, HEAD), ((0, 4),), -0.2, 0.2), 1.0, 2.0),
        "modulation": gaussian(seeds[5], (N_SECTION, STEPS, 3, D), 1.0, 5.0, ((0, 4),), jnp.float32),
        "patch_order": jax.random.permutation(part_splits[6], N_SECTION).astype(jnp.int32),
        "timestep": plant(jax.random.randint(part_splits[7], (N_SECTION,), 0, STEPS), jax.random.fold_in(part_splits[7], 1), 0, STEPS - 1).astype(jnp.int32),
    }


def layer_norm(values_in):
    center = values_in - lax.optimization_barrier(jnp.mean(values_in, axis=-1, keepdims=True))
    spread = lax.optimization_barrier(jnp.mean(center * center, axis=-1, keepdims=True))
    return center * lax.rsqrt(spread + 1e-06)

def head_norm(values_in, gain):
    square = lax.optimization_barrier(jnp.mean(values_in * values_in, axis=-1, keepdims=True))
    return values_in * lax.rsqrt(square + 1e-06) * gain

def section_block(hidden, cache, w_qkv, w_out, norm_gain, modulation, patch_index, step_index):
    modulate = lax.dynamic_index_in_dim(modulation, step_index.astype(jnp.int32), 0, keepdims=False)
    rows_in = hidden.astype(jnp.float32)
    normed = (layer_norm(rows_in) * (1.0 + modulate[1]) + modulate[0]).astype(jnp.bfloat16)
    projected = jnp.dot(normed, w_qkv.reshape(D, 3 * D), preferred_element_type=jnp.float32).astype(jnp.bfloat16)
    projected = projected.reshape(T_PATCH, 3, HEADS, HEAD)
    queries = head_norm(projected[:, 0].astype(jnp.float32), norm_gain[0]).astype(jnp.bfloat16)
    key_rows = head_norm(projected[:, 1].astype(jnp.float32), norm_gain[1]).astype(jnp.bfloat16)
    fresh = jnp.stack([key_rows.reshape(T_PATCH, D), projected[:, 2].reshape(T_PATCH, D)], axis=1)
    zero = jnp.zeros((), jnp.int32)
    merged = lax.dynamic_update_slice(cache, fresh[None], (patch_index.astype(jnp.int32), zero, zero, zero))
    group_count = T_PATCH // TOK_DEV
    all_keys = merged[:, :, 0].reshape(LENGTH, HEADS, HEAD).astype(jnp.float32)
    all_values = merged[:, :, 1].reshape(PATCHES, group_count, TOK_DEV, HEADS, HEAD).astype(jnp.float32)
    scores = jnp.einsum('thd,shd->hts', queries.astype(jnp.float32), all_keys) / math.sqrt(HEAD)
    top = lax.optimization_barrier(jnp.max(scores, axis=-1, keepdims=True))
    rounded = jnp.exp(scores - top).astype(jnp.bfloat16)
    weights = lax.optimization_barrier(rounded).astype(jnp.float32)
    weights = weights.reshape(HEADS, T_PATCH, PATCHES, group_count, TOK_DEV)
    partial_den = lax.optimization_barrier(jnp.sum(weights, axis=(2, 4))).astype(jnp.bfloat16)
    denominator = lax.optimization_barrier(jnp.sum(lax.optimization_barrier(partial_den).astype(jnp.float32), axis=-1))
    partial_num = jnp.einsum('htpgk,pgkhd->gthd', weights, all_values).astype(jnp.bfloat16)
    numerator = lax.optimization_barrier(jnp.sum(lax.optimization_barrier(partial_num).astype(jnp.float32), axis=0))
    attention = (numerator / denominator.T[:, :, None]).astype(jnp.bfloat16).reshape(T_PATCH, D)
    attn_out = jnp.dot(attention, w_out, preferred_element_type=jnp.float32).astype(jnp.bfloat16)
    block = (rows_in + modulate[2] * attn_out.astype(jnp.float32)).astype(jnp.bfloat16)
    return (block, fresh)

def reference(hidden, kv_cache, w_qkv, w_out, norm_gain, modulation, patch_order, timestep):

    def one_section(packed):
        return section_block(*packed)
    blocks, fresh_kv = lax.map(one_section, (hidden, kv_cache, w_qkv, w_out, norm_gain, modulation, patch_order, timestep))
    next_hidden = jnp.roll(blocks, 1, axis=0)
    return (next_hidden, fresh_kv)
```

```python
import functools
import math

import jax
import jax.numpy as jnp
from jax import lax
from jax.experimental import pallas as pl
from jax.experimental.pallas import tpu as pltpu
from jax.sharding import PartitionSpec as P


def passed_along(array, axis, by):
    count = lax.axis_size(axis)
    return lax.ppermute(array, axis, [(i, (i + by) % count) for i in range(count)])


def layer_norm(values_in):
    center = values_in - jnp.mean(values_in, axis=-1, keepdims=True)
    spread = jnp.mean(center * center, axis=-1, keepdims=True)
    return center * lax.rsqrt(spread + 1e-06)


def head_norm(values_in, gain):
    square = jnp.mean(values_in * values_in, axis=-1, keepdims=True)
    return values_in * lax.rsqrt(square + 1e-06) * gain


def body(hidden, kv_cache, w_qkv, w_out, norm_gain, modulation, patch_order, timestep):
    section_index = lax.axis_index("section")
    patch_index = lax.dynamic_index_in_dim(patch_order, section_index, 0, keepdims=False)
    step_index = lax.dynamic_index_in_dim(timestep, section_index, 0, keepdims=False)
    modulate = lax.dynamic_index_in_dim(modulation[0], step_index, 0, keepdims=False)
    model_width = hidden.shape[2]
    head_size = norm_gain.shape[2]
    head_count = model_width // head_size
    col_width = w_qkv.shape[3]
    rows_in = hidden[0].astype(jnp.float32)
    own_count = rows_in.shape[0]
    normed = (layer_norm(rows_in) * (1.0 + modulate[1]) + modulate[0]).astype(jnp.bfloat16)
    w_local = w_qkv[0].reshape(model_width, 3 * col_width)
    projected = jnp.dot(
        lax.all_gather(normed, "seq", axis=0, tiled=True),
        w_local,
        preferred_element_type=jnp.float32,
    ).astype(jnp.bfloat16)
    patch_len = projected.shape[0]
    projected = projected.reshape(patch_len, 3, col_width)
    query_cols = lax.all_gather(projected[:, 0], "seq", axis=1, tiled=True)
    kv_rows = lax.all_to_all(projected[:, 1:], "seq", split_axis=0, concat_axis=2, tiled=True)
    queries = head_norm(
        query_cols.astype(jnp.float32).reshape(patch_len, head_count, head_size), norm_gain[0, 0]
    ).astype(jnp.bfloat16)
    key_rows = head_norm(
        kv_rows[:, 0].astype(jnp.float32).reshape(own_count, head_count, head_size), norm_gain[0, 1]
    ).astype(jnp.bfloat16)
    fresh = jnp.stack([key_rows.reshape(own_count, model_width), kv_rows[:, 1]], axis=1)
    zero = jnp.zeros((), jnp.int32)
    local_kv = lax.dynamic_update_slice(kv_cache[0], fresh[None], (patch_index, zero, zero, zero))
    patch_count = local_kv.shape[0]
    local_keys = local_kv[:, :, 0].reshape(patch_count * own_count, head_count, head_size)
    local_values = local_kv[:, :, 1].reshape(patch_count * own_count, head_count, head_size)
    scores = jnp.einsum(
        "thd,shd->hts", queries, local_keys, preferred_element_type=jnp.float32
    ) / math.sqrt(head_size)
    row_top = lax.pmax(jnp.max(scores, axis=-1), "seq")
    weights = jnp.exp(scores - row_top[:, :, None]).astype(jnp.bfloat16)
    denominator = jnp.sum(weights, axis=-1, dtype=jnp.float32).T
    numerator = jnp.einsum(
        "hts,shd->thd", weights, local_values, preferred_element_type=jnp.float32
    ).reshape(patch_len, model_width)
    totals, counts = (
        lax.psum(numerator.astype(jnp.bfloat16), "seq").astype(jnp.float32),
        lax.psum(denominator.astype(jnp.bfloat16), "seq").astype(jnp.float32),
    )
    attention = (totals.reshape(patch_len, head_count, head_size) / counts[:, :, None]).astype(
        jnp.bfloat16
    )
    attention = attention.reshape(patch_len, model_width)
    out_cols = jnp.dot(attention, w_out[0], preferred_element_type=jnp.float32).astype(jnp.bfloat16)
    out_rows = lax.all_to_all(out_cols, "seq", split_axis=0, concat_axis=1, tiled=True)
    block = (rows_in + modulate[2] * out_rows.astype(jnp.float32)).astype(jnp.bfloat16)
    arrived = passed_along(block, "section", 1)
    return (arrived[None], fresh[None])


MESH = pl.DeviceIdType.MESH


def fused_kernel(
    n, sections, chunk,
    patch_ref, step_ref, hidden_hbm, cache_hbm, qkv_hbm, out_hbm, gain_hbm, mod_hbm,
    next_hbm, fresh_hbm,
    h_buf, rows_f32, normed, cache_buf, keys, values, w_qkv, w_out, gain, mod,
    fresh_stage, att_buf, block_stage,
    sem_qkv, sem_out, sem_small, sem_own, hid_s, hid_r, cache_s, cache_r, fresh_s, fresh_r,
    att_s, att_r, blk_s, blk_r,
):
    f32, bf16 = jnp.float32, jnp.bfloat16
    me = lax.axis_index("seq")
    section = lax.axis_index("section")
    after = lax.rem(section + 1, sections)
    before = lax.rem(section + sections - 1, sections)
    tokens, width = h_buf.shape[1], h_buf.shape[2]
    cols = w_qkv.shape[2]
    patches = cache_buf.shape[1]
    head = gain.shape[2]
    heads = cols // head
    rows = n * tokens
    stale = n * patches * tokens
    parts = width // chunk

    def cols_of(index):
        return pl.ds(pl.multiple_of(index * cols, head), cols)

    def peer(step):
        return lax.rem(me + step, n)

    def origin(step):
        return lax.rem(me + n - step, n)

    own_hidden = pltpu.make_async_copy(hidden_hbm.at[0], h_buf.at[me], sem_own.at[0])
    own_hidden.start()
    small = [
        pltpu.make_async_copy(gain_hbm, gain, sem_small.at[0]),
        pltpu.make_async_copy(mod_hbm, mod, sem_small.at[1]),
    ]
    for copy in small:
        copy.start()
    own_cache = pltpu.make_async_copy(
        cache_hbm.at[0, :, :, :, cols_of(me)], cache_buf.at[me], sem_own.at[1]
    )
    own_cache.start()
    qkv_copies = {}
    for which in (1, 0, 2):
        for part in range(parts):
            span = pl.ds(part * chunk, chunk)
            qkv_copies[which, part] = pltpu.make_async_copy(
                qkv_hbm.at[which, span], w_qkv.at[which, span], sem_qkv.at[which, part]
            )

    barrier = pltpu.get_barrier_semaphore()
    for step in range(1, n):
        pl.semaphore_signal(
            barrier, inc=1, device_id={"seq": peer(step)}, device_id_type=MESH
        )
    for index in range(n):
        pl.semaphore_signal(
            barrier, inc=1, device_id={"section": before, "seq": index}, device_id_type=MESH
        )
    for part in range(parts):
        qkv_copies[1, part].start()
    pl.semaphore_wait(barrier, 2 * n - 1)

    sends = []

    def send(src, dst, send_sem, recv_sem, device):
        copy = pltpu.make_async_remote_copy(
            src_ref=src, dst_ref=dst, send_sem=send_sem, recv_sem=recv_sem,
            device_id=device, device_id_type=MESH,
        )
        copy.start()
        sends.append(copy)

    def arrival(dst, send_sem, recv_sem, device):
        pltpu.make_async_remote_copy(
            src_ref=dst, dst_ref=dst, send_sem=send_sem, recv_sem=recv_sem,
            device_id=device, device_id_type=MESH,
        ).wait_recv()

    for step in range(1, n):
        send(
            hidden_hbm.at[0], h_buf.at[me], hid_s.at[step], hid_r.at[me], {"seq": peer(step)}
        )
    for step in range(1, n):
        send(
            cache_hbm.at[0, :, :, :, cols_of(peer(step))], cache_buf.at[me],
            cache_s.at[step], cache_r.at[me], {"seq": peer(step)},
        )
    for which in (0, 2):
        for part in range(parts):
            qkv_copies[which, part].start()
    out_copies = [
        pltpu.make_async_copy(out_hbm.at[index], w_out.at[index], sem_out.at[index])
        for index in range(n)
    ]
    for copy in out_copies:
        copy.start()

    for copy in small:
        copy.wait()
    step_index = step_ref[section]
    chosen = lax.broadcasted_iota(jnp.int32, (mod.shape[1], 1), 0) == step_index
    shift, scale, gate = (
        jnp.sum(jnp.where(chosen, mod[which], 0.0), axis=0, keepdims=True) for which in range(3)
    )
    block_gate = jnp.sum(
        jnp.where(chosen, mod[2, :, cols_of(me)], 0.0), axis=0, keepdims=True
    )
    own_hidden.wait()
    for step in range(1, n):
        arrival(
            h_buf.at[origin(step)], hid_s.at[step], hid_r.at[origin(step)],
            {"seq": origin(step)},
        )
    for index in range(n):
        rows_f32[index * tokens : (index + 1) * tokens, :] = h_buf[index].astype(f32)
    rows_in = rows_f32[...]
    center = rows_in - jnp.mean(rows_in, axis=-1, keepdims=True)
    spread = jnp.mean(center * center, axis=-1, keepdims=True)
    normed[...] = (center * lax.rsqrt(spread + 1e-06) * (1.0 + scale) + shift).astype(bf16)

    own_cache.wait()
    for step in range(1, n):
        arrival(
            cache_buf.at[origin(step)], cache_s.at[step], cache_r.at[origin(step)],
            {"seq": origin(step)},
        )
    per = patches * tokens
    for index in range(n):
        pair = cache_buf[index].astype(f32).reshape(per, 2, cols)
        keys[index * per : (index + 1) * per, :] = pair[:, 0, :].astype(bf16)
        values[index * per : (index + 1) * per, :] = pair[:, 1, :].astype(bf16)

    def project(which):
        total = jnp.zeros((rows, cols), f32)
        for part in range(parts):
            qkv_copies[which, part].wait()
            span = slice(part * chunk, (part + 1) * chunk)
            total += jnp.dot(normed[:, span], w_qkv[which, span, :], preferred_element_type=f32)
        return total.astype(bf16)

    def head_norms(projected, which):
        done = []
        for index in range(heads):
            vector = projected[:, index * head : (index + 1) * head].astype(f32)
            square = jnp.mean(vector * vector, axis=-1, keepdims=True)
            done.append((vector * lax.rsqrt(square + 1e-06) * gain[0, which : which + 1, :]).astype(bf16))
        return done

    fresh_keys = head_norms(project(1), 1)
    for index in range(heads):
        keys[stale:, index * head : (index + 1) * head] = fresh_keys[index]
    queries = head_norms(project(0), 0)

    count = stale + rows
    column = lax.broadcasted_iota(jnp.int32, (1, count), 1)
    is_cache = column < stale
    in_patch = lax.rem(column // tokens, patches)
    replaced = jnp.logical_and(is_cache, in_patch == patch_ref[section])
    group = jnp.where(is_cache, column // per, (column - stale) // tokens)
    row_group = lax.broadcasted_iota(jnp.int32, (n * rows, 1), 0) // rows
    same_group = row_group == group
    weights, counts = [], []
    for index in range(heads):
        scores = lax.dot_general(
            queries[index], keys[:, index * head : (index + 1) * head],
            (((1,), (1,)), ((), ())), preferred_element_type=f32,
        ) * (1.0 / math.sqrt(head))
        scores = jnp.where(replaced, -jnp.inf, scores)
        top = jnp.max(scores, axis=-1, keepdims=True)
        weight = jnp.exp(scores - top).astype(bf16).astype(f32)
        grouped = jnp.where(same_group, jnp.concatenate([weight] * n, axis=0), 0.0)
        partial = jnp.sum(grouped, axis=-1, keepdims=True).astype(bf16).astype(f32)
        counts.append(sum(partial[i * rows : (i + 1) * rows] for i in range(n)))
        weights.append(grouped.astype(bf16))

    fresh_values = project(2)
    values[stale:, :] = fresh_values
    for index in range(heads):
        span = slice(index * head, (index + 1) * head)
        partial = jnp.dot(weights[index], values[:, span], preferred_element_type=f32)
        partial = partial.astype(bf16).astype(f32)
        numerator = sum(partial[i * rows : (i + 1) * rows] for i in range(n))
        att_buf[me, :, span] = (numerator / counts[index]).astype(bf16)
    for step in range(1, n):
        send(
            att_buf.at[me], att_buf.at[me], att_s.at[step], att_r.at[me], {"seq": peer(step)}
        )

    keys_f32 = keys[stale:, :].astype(f32)
    values_f32 = fresh_values.astype(f32)
    for index in range(n):
        span = slice(index * tokens, (index + 1) * tokens)
        which = lax.broadcasted_iota(jnp.int32, (tokens, 2, cols), 1)
        fresh_stage[index] = jnp.where(
            which == 0, keys_f32[span][:, None, :], values_f32[span][:, None, :]
        ).astype(bf16)
    own_fresh = pltpu.make_async_copy(
        fresh_stage.at[me], fresh_hbm.at[0, :, :, cols_of(me)], sem_own.at[2]
    )
    own_fresh.start()
    for step in range(1, n):
        send(
            fresh_stage.at[peer(step)], fresh_hbm.at[0, :, :, cols_of(me)],
            fresh_s.at[step], fresh_r.at[me], {"seq": peer(step)},
        )

    for copy in out_copies:
        copy.wait()
    total = jnp.dot(att_buf[me], w_out[me], preferred_element_type=f32)
    for step in range(1, n):
        source = origin(step)
        arrival(att_buf.at[source], att_s.at[step], att_r.at[source], {"seq": source})
        total += jnp.dot(att_buf[source], w_out[source], preferred_element_type=f32)
    attn_out = total.astype(bf16).astype(f32)
    block = rows_f32[:, cols_of(me)] + block_gate * attn_out
    for index in range(n):
        block_stage[index] = block[index * tokens : (index + 1) * tokens].astype(bf16)
    for index in range(n):
        send(
            block_stage.at[index], next_hbm.at[0, :, cols_of(me)],
            blk_s.at[index], blk_r.at[me], {"section": after, "seq": index},
        )
    own_fresh.wait()
    for step in range(1, n):
        source = origin(step)
        arrival(
            fresh_hbm.at[0, :, :, cols_of(source)], fresh_s.at[step], fresh_r.at[source],
            {"seq": source},
        )
    for index in range(n):
        arrival(
            next_hbm.at[0, :, cols_of(index)], blk_s.at[index], blk_r.at[index],
            {"section": before, "seq": index},
        )
    for copy in sends:
        copy.wait_send()


def fused(hidden, kv_cache, w_qkv, w_out, norm_gain, modulation, patch_order, timestep):
    n = lax.axis_size("seq")
    sections = lax.axis_size("section")
    tokens, width = hidden.shape[1:]
    patches = kv_cache.shape[1]
    cols = w_qkv.shape[3]
    rows = n * tokens
    stale = n * patches * tokens
    chunk = width // 3 if width % 48 == 0 else width
    parts = width // chunk
    bf16, f32 = jnp.bfloat16, jnp.float32
    anywhere = pl.BlockSpec(memory_space=pl.ANY)
    scalars = pl.BlockSpec(memory_space=pltpu.SMEM)
    dma = pltpu.SemaphoreType.DMA
    return pl.pallas_call(
        functools.partial(fused_kernel, n, sections, chunk),
        out_shape=(
            jax.ShapeDtypeStruct(hidden.shape, bf16),
            jax.ShapeDtypeStruct((1, tokens, 2, width), bf16),
        ),
        in_specs=[scalars] * 2 + [anywhere] * 6,
        out_specs=(anywhere, anywhere),
        scratch_shapes=[
            pltpu.VMEM((n, tokens, width), bf16),
            pltpu.VMEM((rows, width), f32),
            pltpu.VMEM((rows, width), bf16),
            pltpu.VMEM((n, patches, tokens, 2, cols), bf16),
            pltpu.VMEM((stale + rows, cols), bf16),
            pltpu.VMEM((stale + rows, cols), bf16),
            pltpu.VMEM((3, width, cols), bf16),
            pltpu.VMEM((n, cols, cols), bf16),
            pltpu.VMEM(norm_gain.shape, f32),
            pltpu.VMEM((3, modulation.shape[1], width), f32),
            pltpu.VMEM((n, tokens, 2, cols), bf16),
            pltpu.VMEM((n, rows, cols), bf16),
            pltpu.VMEM((n, tokens, cols), bf16),
            dma((3, parts)),
            dma((n,)),
            dma((2,)),
            dma((3,)),
        ]
        + [dma((n,))] * 10,
        compiler_params=pltpu.CompilerParams(
            collective_id=0, has_side_effects=True, vmem_limit_bytes=50 * 2**20
        ),
    )(
        patch_order,
        timestep,
        hidden,
        kv_cache,
        jnp.transpose(w_qkv[0], (1, 0, 2)),
        w_out[0].reshape(n, cols, cols),
        norm_gain,
        jnp.transpose(modulation[0], (1, 0, 2)),
    )


def block_step(*arrays):
    hidden, w_qkv, norm_gain = arrays[0], arrays[2], arrays[4]
    lanes = norm_gain.shape[2]
    whole_heads = lanes % 128 == 0 and w_qkv.shape[3] % lanes == 0
    whole_tiles = lax.axis_size("seq") * hidden.shape[1] % 16 == 0
    if whole_heads and whole_tiles and lax.axis_size("seq") > 1 and lax.axis_size("section") > 1:
        return fused(*arrays)
    return body(*arrays)


def solution(mesh):
    return jax.shard_map(
        block_step,
        mesh=mesh,
        in_specs=(
            P("section", ("groups", "seq"), None),
            P("section", None, ("groups", "seq"), None, None),
            P("section", None, None, "seq"),
            P("section", None, "seq"),
            P("section", None, None),
            P("section", None, None, None),
            P("groups"),
            P("groups"),
        ),
        out_specs=(
            P("section", ("groups", "seq"), None),
            P("section", ("groups", "seq"), None, None),
        ),
        check_vma=False,
    )
```

```python
import functools
import math

import jax
import jax.numpy as jnp
from jax import lax
from jax.experimental import pallas as pl
from jax.experimental.pallas import tpu as pltpu
from jax.sharding import PartitionSpec as P


def passed_along(array, axis, by):
    count = lax.axis_size(axis)
    return lax.ppermute(array, axis, [(i, (i + by) % count) for i in range(count)])


def layer_norm(values_in):
    center = values_in - jnp.mean(values_in, axis=-1, keepdims=True)
    spread = jnp.mean(center * center, axis=-1, keepdims=True)
    return center * lax.rsqrt(spread + 1e-06)


def head_norm(values_in, gain):
    square = jnp.mean(values_in * values_in, axis=-1, keepdims=True)
    return values_in * lax.rsqrt(square + 1e-06) * gain


def body(hidden, kv_cache, w_qkv, w_out, norm_gain, modulation, patch_order, timestep):
    section_index = lax.axis_index("section")
    patch_index = lax.dynamic_index_in_dim(patch_order, section_index, 0, keepdims=False)
    step_index = lax.dynamic_index_in_dim(timestep, section_index, 0, keepdims=False)
    modulate = lax.dynamic_index_in_dim(modulation[0], step_index, 0, keepdims=False)
    model_width = hidden.shape[2]
    head_size = norm_gain.shape[2]
    head_count = model_width // head_size
    col_width = w_qkv.shape[3]
    rows_in = hidden[0].astype(jnp.float32)
    own_count = rows_in.shape[0]
    normed = (layer_norm(rows_in) * (1.0 + modulate[1]) + modulate[0]).astype(jnp.bfloat16)
    w_local = w_qkv[0].reshape(model_width, 3 * col_width)
    projected = jnp.dot(
        lax.all_gather(normed, "seq", axis=0, tiled=True),
        w_local,
        preferred_element_type=jnp.float32,
    ).astype(jnp.bfloat16)
    patch_len = projected.shape[0]
    projected = projected.reshape(patch_len, 3, col_width)
    query_cols = lax.all_gather(projected[:, 0], "seq", axis=1, tiled=True)
    kv_rows = lax.all_to_all(projected[:, 1:], "seq", split_axis=0, concat_axis=2, tiled=True)
    queries = head_norm(
        query_cols.astype(jnp.float32).reshape(patch_len, head_count, head_size), norm_gain[0, 0]
    ).astype(jnp.bfloat16)
    key_rows = head_norm(
        kv_rows[:, 0].astype(jnp.float32).reshape(own_count, head_count, head_size), norm_gain[0, 1]
    ).astype(jnp.bfloat16)
    fresh = jnp.stack([key_rows.reshape(own_count, model_width), kv_rows[:, 1]], axis=1)
    zero = jnp.zeros((), jnp.int32)
    local_kv = lax.dynamic_update_slice(kv_cache[0], fresh[None], (patch_index, zero, zero, zero))
    patch_count = local_kv.shape[0]
    local_keys = local_kv[:, :, 0].reshape(patch_count * own_count, head_count, head_size)
    local_values = local_kv[:, :, 1].reshape(patch_count * own_count, head_count, head_size)
    scores = jnp.einsum(
        "thd,shd->hts", queries, local_keys, preferred_element_type=jnp.float32
    ) / math.sqrt(head_size)
    row_top = lax.pmax(jnp.max(scores, axis=-1), "seq")
    weights = jnp.exp(scores - row_top[:, :, None]).astype(jnp.bfloat16)
    denominator = jnp.sum(weights, axis=-1, dtype=jnp.float32).T
    numerator = jnp.einsum(
        "hts,shd->thd", weights, local_values, preferred_element_type=jnp.float32
    ).reshape(patch_len, model_width)
    totals, counts = (
        lax.psum(numerator.astype(jnp.bfloat16), "seq").astype(jnp.float32),
        lax.psum(denominator.astype(jnp.bfloat16), "seq").astype(jnp.float32),
    )
    attention = (totals.reshape(patch_len, head_count, head_size) / counts[:, :, None]).astype(
        jnp.bfloat16
    )
    attention = attention.reshape(patch_len, model_width)
    out_cols = jnp.dot(attention, w_out[0], preferred_element_type=jnp.float32).astype(jnp.bfloat16)
    out_rows = lax.all_to_all(out_cols, "seq", split_axis=0, concat_axis=1, tiled=True)
    block = (rows_in + modulate[2] * out_rows.astype(jnp.float32)).astype(jnp.bfloat16)
    arrived = passed_along(block, "section", 1)
    return (arrived[None], fresh[None])


MESH = pl.DeviceIdType.MESH


def fused_kernel(
    n, sections, chunk,
    patch_hbm, step_hbm, hidden_hbm, cache_hbm, qkv_hbm, out_hbm, gain_hbm, mod_hbm,
    next_hbm, fresh_hbm,
    own_rows, hid_cols, norm_buf, rows_f32, own_cache, cache_stage, keys, values, w_qkv, w_out,
    gain, mod, patch, step_at, fresh_stage, att_buf, block_stage,
    sem_qkv, sem_out, sem_small, norm_s, norm_r, hid_s, hid_r, key_s, key_r, value_s, value_r,
    fresh_s, fresh_r, att_s, att_r, blk_s, blk_r,
):
    f32, bf16 = jnp.float32, jnp.bfloat16
    me = lax.axis_index("seq")
    section = lax.axis_index("section")
    after = lax.rem(section + 1, sections)
    before = lax.rem(section + sections - 1, sections)
    tokens, width = own_rows.shape
    cols = w_qkv.shape[2]
    patches = own_cache.shape[0]
    head = gain.shape[2]
    heads = cols // head
    rows = n * tokens
    per = patches * tokens
    stale = n * per
    parts = width // chunk

    def cols_of(index):
        return pl.ds(pl.multiple_of(index * cols, head), cols)

    def per_of(index):
        return pl.ds(pl.multiple_of(index * per, per), per)

    def peer(step):
        return lax.rem(me + step, n)

    def origin(step):
        return lax.rem(me + n - step, n)

    barrier = pltpu.get_barrier_semaphore()
    for step in range(1, n):
        pl.semaphore_signal(
            barrier, inc=1, device_id={"seq": peer(step)}, device_id_type=MESH
        )
    for index in range(n):
        pl.semaphore_signal(
            barrier, inc=1, device_id={"section": before, "seq": index}, device_id_type=MESH
        )
    small = [
        pltpu.make_async_copy(src, dst, sem_small.at[place])
        for place, (src, dst) in enumerate(
            (
                (hidden_hbm.at[0], own_rows),
                (mod_hbm, mod),
                (step_hbm, step_at),
                (patch_hbm, patch),
                (gain_hbm, gain),
                (cache_hbm.at[0], own_cache),
            )
        )
    ]
    for copy in small:
        copy.start()
    qkv_copies = {}
    for which in (1, 0, 2):
        for part in range(parts):
            span = pl.ds(part * chunk, chunk)
            copy = pltpu.make_async_copy(
                qkv_hbm.at[which, span], w_qkv.at[which, span], sem_qkv.at[which, part]
            )
            copy.start()
            qkv_copies[which, part] = copy

    for copy in small[:3]:
        copy.wait()
    chosen = lax.broadcasted_iota(jnp.int32, (mod.shape[1], 1), 0) == step_at[section]
    shift, scale = (
        jnp.sum(jnp.where(chosen, mod[which], 0.0), axis=0, keepdims=True) for which in range(2)
    )
    rows_in = own_rows[...].astype(f32)
    center = rows_in - jnp.mean(rows_in, axis=-1, keepdims=True)
    spread = jnp.mean(center * center, axis=-1, keepdims=True)
    norm_buf[me] = (center * lax.rsqrt(spread + 1e-06) * (1.0 + scale) + shift).astype(bf16)
    pl.semaphore_wait(barrier, 2 * n - 1)

    sends = []

    def send(src, dst, send_sem, recv_sem, device):
        copy = pltpu.make_async_remote_copy(
            src_ref=src, dst_ref=dst, send_sem=send_sem, recv_sem=recv_sem,
            device_id=device, device_id_type=MESH,
        )
        copy.start()
        sends.append(copy)

    def arrival(dst, send_sem, recv_sem, device):
        pltpu.make_async_remote_copy(
            src_ref=dst, dst_ref=dst, send_sem=send_sem, recv_sem=recv_sem,
            device_id=device, device_id_type=MESH,
        ).wait_recv()

    for step in range(1, n):
        send(norm_buf.at[me], norm_buf.at[me], norm_s.at[step], norm_r.at[me], {"seq": peer(step)})

    for copy in small[3:]:
        copy.wait()
    pair = own_cache[...].astype(f32).reshape(per, 2, width)
    for which in range(2):
        split = pair[:, which, :].astype(bf16)
        for index in range(n):
            cache_stage[which, index] = split[:, index * cols : (index + 1) * cols]
    for which, (into, send_sem, recv_sem) in enumerate(
        ((keys, key_s, key_r), (values, value_s, value_r))
    ):
        for step in range(1, n):
            send(
                cache_stage.at[which, peer(step)], into.at[per_of(me)],
                send_sem.at[step], recv_sem.at[me], {"seq": peer(step)},
            )
        into[per_of(me), :] = cache_stage[which, me]
    for step in range(1, n):
        send(
            own_rows.at[:, cols_of(peer(step))], hid_cols.at[me], hid_s.at[step], hid_r.at[me],
            {"seq": peer(step)},
        )
    hid_cols[me] = own_rows[:, cols_of(me)]
    out_copies = [
        pltpu.make_async_copy(out_hbm.at[index], w_out.at[index], sem_out.at[index])
        for index in range(n)
    ]
    for copy in out_copies:
        copy.start()

    for step in range(1, n):
        source = origin(step)
        arrival(norm_buf.at[source], norm_s.at[step], norm_r.at[source], {"seq": source})
    for index in range(n):
        rows_f32[index * tokens : (index + 1) * tokens, :] = norm_buf[index].astype(f32)
    normed = rows_f32[...].astype(bf16)

    def project(which):
        total = jnp.zeros((rows, cols), f32)
        for part in range(parts):
            qkv_copies[which, part].wait()
            span = slice(part * chunk, (part + 1) * chunk)
            total += jnp.dot(normed[:, span], w_qkv[which, span, :], preferred_element_type=f32)
        return total.astype(bf16)

    def head_norms(projected, which):
        done = []
        for index in range(heads):
            vector = projected[:, index * head : (index + 1) * head].astype(f32)
            square = jnp.mean(vector * vector, axis=-1, keepdims=True)
            normal = vector * lax.rsqrt(square + 1e-06) * gain[0, which : which + 1, :]
            done.append(normal.astype(bf16))
        return done

    fresh_keys = jnp.concatenate(head_norms(project(1), 1), axis=1)
    keys[stale:, :] = fresh_keys
    queries = head_norms(project(0), 0)

    for step in range(1, n):
        source = origin(step)
        arrival(keys.at[per_of(source)], key_s.at[step], key_r.at[source], {"seq": source})
        arrival(values.at[per_of(source)], value_s.at[step], value_r.at[source], {"seq": source})
    count = stale + rows
    column = lax.broadcasted_iota(jnp.int32, (1, count), 1)
    is_cache = column < stale
    in_patch = lax.rem(column // tokens, patches)
    replaced = jnp.logical_and(is_cache, in_patch == patch[section])
    group = jnp.where(is_cache, column // per, (column - stale) // tokens)
    row_group = lax.broadcasted_iota(jnp.int32, (n * rows, 1), 0) // rows
    same_group = row_group == group
    weights = []
    for index in range(heads):
        scores = lax.dot_general(
            queries[index], keys[:, index * head : (index + 1) * head],
            (((1,), (1,)), ((), ())), preferred_element_type=f32,
        ) * (1.0 / math.sqrt(head))
        scores = jnp.where(replaced, -jnp.inf, scores)
        top = jnp.max(scores, axis=-1, keepdims=True)
        weight = jnp.exp(scores - top)
        grouped = jnp.where(same_group, jnp.concatenate([weight] * n, axis=0), 0.0)
        weights.append(grouped.astype(bf16))

    fresh_values = project(2)
    values[stale:, :] = fresh_values
    ones = jnp.ones((count, head), bf16)
    for index in range(heads):
        span = slice(index * head, (index + 1) * head)
        both = jnp.concatenate([values[:, span], ones], axis=1)
        partial = jnp.dot(weights[index], both, preferred_element_type=f32)
        partial = partial.astype(bf16).astype(f32)
        sums = sum(partial[i * rows : (i + 1) * rows] for i in range(n))
        att_buf[me, :, span] = (sums[:, :head] / sums[:, head:]).astype(bf16)
    for step in range(1, n):
        send(att_buf.at[me], att_buf.at[me], att_s.at[step], att_r.at[me], {"seq": peer(step)})

    keys_f32 = fresh_keys.astype(f32)
    values_f32 = fresh_values.astype(f32)
    is_key = lax.broadcasted_iota(jnp.int32, (tokens, 2, cols), 1) == 0
    for index in range(n):
        span = slice(index * tokens, (index + 1) * tokens)
        fresh_stage[index] = jnp.where(
            is_key, keys_f32[span][:, None, :], values_f32[span][:, None, :]
        ).astype(bf16)
    own_fresh = pltpu.make_async_copy(
        fresh_stage.at[me], fresh_hbm.at[0, :, :, cols_of(me)], sem_small.at[6]
    )
    own_fresh.start()
    for step in range(1, n):
        send(
            fresh_stage.at[peer(step)], fresh_hbm.at[0, :, :, cols_of(me)],
            fresh_s.at[step], fresh_r.at[me], {"seq": peer(step)},
        )
    gate = jnp.sum(jnp.where(chosen, mod[2, :, cols_of(me)], 0.0), axis=0, keepdims=True)

    for copy in out_copies:
        copy.wait()
    total = jnp.dot(att_buf[me], w_out[me], preferred_element_type=f32)
    for step in range(1, n):
        source = origin(step)
        arrival(att_buf.at[source], att_s.at[step], att_r.at[source], {"seq": source})
        total += jnp.dot(att_buf[source], w_out[source], preferred_element_type=f32)
    for step in range(1, n):
        source = origin(step)
        arrival(hid_cols.at[source], hid_s.at[step], hid_r.at[source], {"seq": source})
    change = gate * total.astype(bf16).astype(f32)
    for index in range(n):
        block = hid_cols[index].astype(f32) + change[index * tokens : (index + 1) * tokens]
        block_stage[index] = block.astype(bf16)
    for index in range(n):
        send(
            block_stage.at[index], next_hbm.at[0, :, cols_of(me)],
            blk_s.at[index], blk_r.at[me], {"section": after, "seq": index},
        )
    own_fresh.wait()
    for step in range(1, n):
        source = origin(step)
        arrival(
            fresh_hbm.at[0, :, :, cols_of(source)], fresh_s.at[step], fresh_r.at[source],
            {"seq": source},
        )
    for index in range(n):
        arrival(
            next_hbm.at[0, :, cols_of(index)], blk_s.at[index], blk_r.at[index],
            {"section": before, "seq": index},
        )
    for copy in sends:
        copy.wait_send()


def fused(hidden, kv_cache, w_qkv, w_out, norm_gain, modulation, patch_order, timestep):
    n = lax.axis_size("seq")
    sections = lax.axis_size("section")
    tokens, width = hidden.shape[1:]
    patches = kv_cache.shape[1]
    cols = w_qkv.shape[3]
    rows = n * tokens
    per = patches * tokens
    chunk = width // 3 if width % 48 == 0 else width
    parts = width // chunk
    bf16, f32 = jnp.bfloat16, jnp.float32
    anywhere = pl.BlockSpec(memory_space=pl.ANY)
    in_hbm = pl.BlockSpec(memory_space=pltpu.HBM)
    dma = pltpu.SemaphoreType.DMA
    return pl.pallas_call(
        functools.partial(fused_kernel, n, sections, chunk),
        out_shape=(
            jax.ShapeDtypeStruct(hidden.shape, bf16),
            jax.ShapeDtypeStruct((1, tokens, 2, width), bf16),
        ),
        in_specs=[in_hbm] * 8,
        out_specs=(anywhere, anywhere),
        scratch_shapes=[
            pltpu.VMEM((tokens, width), bf16),
            pltpu.VMEM((n, tokens, cols), bf16),
            pltpu.VMEM((n, tokens, width), bf16),
            pltpu.VMEM((rows, width), f32),
            pltpu.VMEM((patches, tokens, 2, width), bf16),
            pltpu.VMEM((2, n, per, cols), bf16),
            pltpu.VMEM((n * per + rows, cols), bf16),
            pltpu.VMEM((n * per + rows, cols), bf16),
            pltpu.VMEM((3, width, cols), bf16),
            pltpu.VMEM((n, cols, cols), bf16),
            pltpu.VMEM(norm_gain.shape, f32),
            pltpu.VMEM((3, modulation.shape[1], width), f32),
            pltpu.SMEM(patch_order.shape, jnp.int32),
            pltpu.SMEM(timestep.shape, jnp.int32),
            pltpu.VMEM((n, tokens, 2, cols), bf16),
            pltpu.VMEM((n, rows, cols), bf16),
            pltpu.VMEM((n, tokens, cols), bf16),
            dma((3, parts)),
            dma((n,)),
            dma((7,)),
        ]
        + [dma((n,))] * 14,
        compiler_params=pltpu.CompilerParams(
            collective_id=0, has_side_effects=True, vmem_limit_bytes=60 * 2**20
        ),
    )(
        patch_order,
        timestep,
        hidden,
        kv_cache,
        jnp.transpose(w_qkv[0], (1, 0, 2)),
        w_out[0].reshape(n, cols, cols),
        norm_gain,
        jnp.transpose(modulation[0], (1, 0, 2)),
    )


def block_step(*arrays):
    hidden, w_qkv, norm_gain = arrays[0], arrays[2], arrays[4]
    lanes = norm_gain.shape[2]
    whole_heads = lanes % 128 == 0 and w_qkv.shape[3] % lanes == 0
    rows, per = lax.axis_size("seq") * hidden.shape[1], arrays[1].shape[1] * hidden.shape[1]
    whole_tiles = rows % 16 == 0 and per % 16 == 0
    if whole_heads and whole_tiles and lax.axis_size("seq") > 1 and lax.axis_size("section") > 1:
        return fused(*arrays)
    return body(*arrays)


def solution(mesh):
    return jax.shard_map(
        block_step,
        mesh=mesh,
        in_specs=(
            P("section", ("groups", "seq"), None),
            P("section", None, ("groups", "seq"), None, None),
            P("section", None, None, "seq"),
            P("section", None, "seq"),
            P("section", None, None),
            P("section", None, None, None),
            P("groups"),
            P("groups"),
        ),
        out_specs=(
            P("section", ("groups", "seq"), None),
            P("section", ("groups", "seq"), None, None),
        ),
        check_vma=False,
    )
```

```python
import functools
import math

import jax
import jax.numpy as jnp
from jax import lax
from jax.experimental import pallas as pl
from jax.experimental.pallas import tpu as pltpu
from jax.sharding import PartitionSpec as P


def passed_along(array, axis, by):
    count = lax.axis_size(axis)
    return lax.ppermute(array, axis, [(i, (i + by) % count) for i in range(count)])


def layer_norm(values_in):
    center = values_in - jnp.mean(values_in, axis=-1, keepdims=True)
    spread = jnp.mean(center * center, axis=-1, keepdims=True)
    return center * lax.rsqrt(spread + 1e-06)


def head_norm(values_in, gain):
    square = jnp.mean(values_in * values_in, axis=-1, keepdims=True)
    return values_in * lax.rsqrt(square + 1e-06) * gain


def body(hidden, kv_cache, w_qkv, w_out, norm_gain, modulation, patch_order, timestep):
    section_index = lax.axis_index("section")
    patch_index = lax.dynamic_index_in_dim(patch_order, section_index, 0, keepdims=False)
    step_index = lax.dynamic_index_in_dim(timestep, section_index, 0, keepdims=False)
    modulate = lax.dynamic_index_in_dim(modulation[0], step_index, 0, keepdims=False)
    model_width = hidden.shape[2]
    head_size = norm_gain.shape[2]
    head_count = model_width // head_size
    col_width = w_qkv.shape[3]
    rows_in = hidden[0].astype(jnp.float32)
    own_count = rows_in.shape[0]
    normed = (layer_norm(rows_in) * (1.0 + modulate[1]) + modulate[0]).astype(jnp.bfloat16)
    w_local = w_qkv[0].reshape(model_width, 3 * col_width)
    projected = jnp.dot(
        lax.all_gather(normed, "seq", axis=0, tiled=True),
        w_local,
        preferred_element_type=jnp.float32,
    ).astype(jnp.bfloat16)
    patch_len = projected.shape[0]
    projected = projected.reshape(patch_len, 3, col_width)
    query_cols = lax.all_gather(projected[:, 0], "seq", axis=1, tiled=True)
    kv_rows = lax.all_to_all(projected[:, 1:], "seq", split_axis=0, concat_axis=2, tiled=True)
    queries = head_norm(
        query_cols.astype(jnp.float32).reshape(patch_len, head_count, head_size), norm_gain[0, 0]
    ).astype(jnp.bfloat16)
    key_rows = head_norm(
        kv_rows[:, 0].astype(jnp.float32).reshape(own_count, head_count, head_size), norm_gain[0, 1]
    ).astype(jnp.bfloat16)
    fresh = jnp.stack([key_rows.reshape(own_count, model_width), kv_rows[:, 1]], axis=1)
    zero = jnp.zeros((), jnp.int32)
    local_kv = lax.dynamic_update_slice(kv_cache[0], fresh[None], (patch_index, zero, zero, zero))
    patch_count = local_kv.shape[0]
    local_keys = local_kv[:, :, 0].reshape(patch_count * own_count, head_count, head_size)
    local_values = local_kv[:, :, 1].reshape(patch_count * own_count, head_count, head_size)
    scores = jnp.einsum(
        "thd,shd->hts", queries, local_keys, preferred_element_type=jnp.float32
    ) / math.sqrt(head_size)
    row_top = lax.pmax(jnp.max(scores, axis=-1), "seq")
    weights = jnp.exp(scores - row_top[:, :, None]).astype(jnp.bfloat16)
    denominator = jnp.sum(weights, axis=-1, dtype=jnp.float32).T
    numerator = jnp.einsum(
        "hts,shd->thd", weights, local_values, preferred_element_type=jnp.float32
    ).reshape(patch_len, model_width)
    totals, counts = (
        lax.psum(numerator.astype(jnp.bfloat16), "seq").astype(jnp.float32),
        lax.psum(denominator.astype(jnp.bfloat16), "seq").astype(jnp.float32),
    )
    attention = (totals.reshape(patch_len, head_count, head_size) / counts[:, :, None]).astype(
        jnp.bfloat16
    )
    attention = attention.reshape(patch_len, model_width)
    out_cols = jnp.dot(attention, w_out[0], preferred_element_type=jnp.float32).astype(jnp.bfloat16)
    out_rows = lax.all_to_all(out_cols, "seq", split_axis=0, concat_axis=1, tiled=True)
    block = (rows_in + modulate[2] * out_rows.astype(jnp.float32)).astype(jnp.bfloat16)
    arrived = passed_along(block, "section", 1)
    return (arrived[None], fresh[None])


MESH = pl.DeviceIdType.MESH


def fused_kernel(
    n, sections, chunk,
    patch_hbm, step_hbm, hidden_hbm, cache_hbm, qkv_hbm, out_hbm, gain_hbm, mod_hbm,
    next_hbm, fresh_hbm,
    own_rows, hid_cols, norm_buf, rows_f32, own_cache, cache_stage, keys, values, w_qkv, w_out,
    gain, mod, patch, step_at, fresh_stage, att_buf, block_stage,
    sem_qkv, sem_out, sem_small, norm_s, norm_r, hid_s, hid_r, key_s, key_r, value_s, value_r,
    fresh_s, fresh_r, att_s, att_r, blk_s, blk_r,
):
    f32, bf16 = jnp.float32, jnp.bfloat16
    me = lax.axis_index("seq")
    section = lax.axis_index("section")
    after = lax.rem(section + 1, sections)
    before = lax.rem(section + sections - 1, sections)
    tokens, width = own_rows.shape
    cols = w_qkv.shape[2]
    patches = own_cache.shape[0]
    head = gain.shape[2]
    heads = cols // head
    rows = n * tokens
    per = patches * tokens
    stale = n * per
    parts = width // chunk

    def cols_of(index):
        return pl.ds(pl.multiple_of(index * cols, head), cols)

    def per_of(index):
        return pl.ds(pl.multiple_of(index * per, per), per)

    upper = me >= n // 2
    edge = jnp.where(upper, n - 1 - me, me)

    def origin(step):
        index = step - 1 + jnp.where(edge <= step - 1, 1, 0)
        return jnp.where(upper, n - 1 - index, index)

    def peer(step):
        return origin(n - step)

    barrier = pltpu.get_barrier_semaphore()
    for step in range(1, n):
        pl.semaphore_signal(
            barrier, inc=1, device_id={"seq": peer(step)}, device_id_type=MESH
        )
    for index in range(n):
        pl.semaphore_signal(
            barrier, inc=1, device_id={"section": before, "seq": index}, device_id_type=MESH
        )
    small = [
        pltpu.make_async_copy(src, dst, sem_small.at[place])
        for place, (src, dst) in enumerate(
            (
                (hidden_hbm.at[0], own_rows),
                (mod_hbm, mod),
                (step_hbm, step_at),
                (patch_hbm, patch),
                (gain_hbm, gain),
                (cache_hbm.at[0], own_cache),
            )
        )
    ]
    for copy in small:
        copy.start()
    qkv_copies = {}
    for part in range(parts):
        for which in (1, 0, 2):
            span = pl.ds(part * chunk, chunk)
            copy = pltpu.make_async_copy(
                qkv_hbm.at[which, span], w_qkv.at[which, span], sem_qkv.at[which, part]
            )
            copy.start()
            qkv_copies[which, part] = copy

    for copy in small[:3]:
        copy.wait()
    chosen = lax.broadcasted_iota(jnp.int32, (mod.shape[1], 1), 0) == step_at[section]
    shift, scale = (
        jnp.sum(jnp.where(chosen, mod[which], 0.0), axis=0, keepdims=True) for which in range(2)
    )
    rows_in = own_rows[...].astype(f32)
    center = rows_in - jnp.mean(rows_in, axis=-1, keepdims=True)
    spread = jnp.mean(center * center, axis=-1, keepdims=True)
    norm_buf[me] = (center * lax.rsqrt(spread + 1e-06) * (1.0 + scale) + shift).astype(bf16)
    pl.semaphore_wait(barrier, 2 * n - 1)

    sends = []

    def send(src, dst, send_sem, recv_sem, device):
        copy = pltpu.make_async_remote_copy(
            src_ref=src, dst_ref=dst, send_sem=send_sem, recv_sem=recv_sem,
            device_id=device, device_id_type=MESH,
        )
        copy.start()
        sends.append(copy)

    def arrival(dst, send_sem, recv_sem, device):
        pltpu.make_async_remote_copy(
            src_ref=dst, dst_ref=dst, send_sem=send_sem, recv_sem=recv_sem,
            device_id=device, device_id_type=MESH,
        ).wait_recv()

    for part in range(parts):
        piece = norm_buf.at[me, :, pl.ds(part * chunk, chunk)]
        for step in range(1, n):
            send(piece, piece, norm_s.at[part, step], norm_r.at[part, me], {"seq": peer(step)})

    for copy in small[3:]:
        copy.wait()
    pair = own_cache[...].astype(f32).reshape(per, 2, width)
    for which in range(2):
        split = pair[:, which, :].astype(bf16)
        for index in range(n):
            cache_stage[which, index] = split[:, index * cols : (index + 1) * cols]
    for which, (into, send_sem, recv_sem) in enumerate(
        ((keys, key_s, key_r), (values, value_s, value_r))
    ):
        for step in range(1, n):
            send(
                cache_stage.at[which, peer(step)], into.at[per_of(me)],
                send_sem.at[step], recv_sem.at[me], {"seq": peer(step)},
            )
        into[per_of(me), :] = cache_stage[which, me]
    for step in range(1, n):
        send(
            own_rows.at[:, cols_of(peer(step))], hid_cols.at[me], hid_s.at[step], hid_r.at[me],
            {"seq": peer(step)},
        )
    hid_cols[me] = own_rows[:, cols_of(me)]
    out_copies = [
        pltpu.make_async_copy(out_hbm.at[index], w_out.at[index], sem_out.at[index])
        for index in range(n)
    ]
    for copy in out_copies:
        copy.start()

    totals = [jnp.zeros((rows, cols), f32)] * 3
    for part in range(parts):
        span = slice(part * chunk, (part + 1) * chunk)
        for step in range(1, n):
            source = origin(step)
            arrival(
                norm_buf.at[source, :, pl.ds(part * chunk, chunk)],
                norm_s.at[part, step], norm_r.at[part, source], {"seq": source},
            )
        for index in range(n):
            rows_f32[index * tokens : (index + 1) * tokens, span] = norm_buf[index, :, span].astype(
                f32
            )
        normed = rows_f32[:, span].astype(bf16)
        for which in (1, 0, 2):
            qkv_copies[which, part].wait()
            totals[which] += jnp.dot(
                normed, w_qkv[which, span, :], preferred_element_type=f32
            )
    projected = [total.astype(bf16) for total in totals]

    def head_norms(projected, which):
        done = []
        for index in range(heads):
            vector = projected[:, index * head : (index + 1) * head].astype(f32)
            square = jnp.mean(vector * vector, axis=-1, keepdims=True)
            normal = vector * lax.rsqrt(square + 1e-06) * gain[0, which : which + 1, :]
            done.append(normal.astype(bf16))
        return done

    fresh_keys = jnp.concatenate(head_norms(projected[1], 1), axis=1)
    keys[stale:, :] = fresh_keys
    queries = head_norms(projected[0], 0)

    for step in range(1, n):
        source = origin(step)
        arrival(keys.at[per_of(source)], key_s.at[step], key_r.at[source], {"seq": source})
    count = stale + rows
    column = lax.broadcasted_iota(jnp.int32, (1, count), 1)
    is_cache = column < stale
    in_patch = lax.rem(column // tokens, patches)
    replaced = jnp.logical_and(is_cache, in_patch == patch[section])
    group = jnp.where(is_cache, column // per, (column - stale) // tokens)
    row_group = lax.broadcasted_iota(jnp.int32, (n * rows, 1), 0) // rows
    same_group = row_group == group
    weights = []
    for index in range(heads):
        scores = lax.dot_general(
            queries[index], keys[:, index * head : (index + 1) * head],
            (((1,), (1,)), ((), ())), preferred_element_type=f32,
        ) * (1.0 / math.sqrt(head))
        scores = jnp.where(replaced, -jnp.inf, scores)
        top = jnp.max(scores, axis=-1, keepdims=True)
        weight = jnp.exp(scores - top)
        grouped = jnp.where(same_group, jnp.concatenate([weight] * n, axis=0), 0.0)
        weights.append(grouped.astype(bf16))

    fresh_values = projected[2]
    values[stale:, :] = fresh_values
    for step in range(1, n):
        source = origin(step)
        arrival(values.at[per_of(source)], value_s.at[step], value_r.at[source], {"seq": source})
    ones = jnp.ones((count, head), bf16)
    for index in range(heads):
        span = slice(index * head, (index + 1) * head)
        both = jnp.concatenate([values[:, span], ones], axis=1)
        partial = jnp.dot(weights[index], both, preferred_element_type=f32)
        partial = partial.astype(bf16).astype(f32)
        sums = sum(partial[i * rows : (i + 1) * rows] for i in range(n))
        att_buf[me, :, span] = (sums[:, :head] / sums[:, head:]).astype(bf16)
    for step in range(1, n):
        send(att_buf.at[me], att_buf.at[me], att_s.at[step], att_r.at[me], {"seq": peer(step)})

    keys_f32 = fresh_keys.astype(f32)
    values_f32 = fresh_values.astype(f32)
    is_key = lax.broadcasted_iota(jnp.int32, (tokens, 2, cols), 1) == 0
    for index in range(n):
        span = slice(index * tokens, (index + 1) * tokens)
        fresh_stage[index] = jnp.where(
            is_key, keys_f32[span][:, None, :], values_f32[span][:, None, :]
        ).astype(bf16)
    own_fresh = pltpu.make_async_copy(
        fresh_stage.at[me], fresh_hbm.at[0, :, :, cols_of(me)], sem_small.at[6]
    )
    own_fresh.start()
    for step in range(1, n):
        send(
            fresh_stage.at[peer(step)], fresh_hbm.at[0, :, :, cols_of(me)],
            fresh_s.at[step], fresh_r.at[me], {"seq": peer(step)},
        )
    gate = jnp.sum(jnp.where(chosen, mod[2, :, cols_of(me)], 0.0), axis=0, keepdims=True)

    for copy in out_copies:
        copy.wait()
    total = jnp.dot(att_buf[me], w_out[me], preferred_element_type=f32)
    for step in range(1, n):
        source = origin(step)
        arrival(att_buf.at[source], att_s.at[step], att_r.at[source], {"seq": source})
        total += jnp.dot(att_buf[source], w_out[source], preferred_element_type=f32)
    for step in range(1, n):
        source = origin(step)
        arrival(hid_cols.at[source], hid_s.at[step], hid_r.at[source], {"seq": source})
    change = gate * total.astype(bf16).astype(f32)
    for index in range(n):
        block = hid_cols[index].astype(f32) + change[index * tokens : (index + 1) * tokens]
        block_stage[index] = block.astype(bf16)
    for index in range(n):
        send(
            block_stage.at[index], next_hbm.at[0, :, cols_of(me)],
            blk_s.at[index], blk_r.at[me], {"section": after, "seq": index},
        )
    own_fresh.wait()
    for step in range(1, n):
        source = origin(step)
        arrival(
            fresh_hbm.at[0, :, :, cols_of(source)], fresh_s.at[step], fresh_r.at[source],
            {"seq": source},
        )
    for index in range(n):
        arrival(
            next_hbm.at[0, :, cols_of(index)], blk_s.at[index], blk_r.at[index],
            {"section": before, "seq": index},
        )
    for copy in sends:
        copy.wait_send()


def fused(hidden, kv_cache, w_qkv, w_out, norm_gain, modulation, patch_order, timestep):
    n = lax.axis_size("seq")
    sections = lax.axis_size("section")
    tokens, width = hidden.shape[1:]
    patches = kv_cache.shape[1]
    cols = w_qkv.shape[3]
    rows = n * tokens
    per = patches * tokens
    chunk = width // 3 if width % 48 == 0 else width
    parts = width // chunk
    bf16, f32 = jnp.bfloat16, jnp.float32
    anywhere = pl.BlockSpec(memory_space=pl.ANY)
    in_hbm = pl.BlockSpec(memory_space=pltpu.HBM)
    dma = pltpu.SemaphoreType.DMA
    return pl.pallas_call(
        functools.partial(fused_kernel, n, sections, chunk),
        out_shape=(
            pltpu.VMEM(hidden.shape, bf16),
            pltpu.VMEM((1, tokens, 2, width), bf16),
        ),
        in_specs=[in_hbm] * 8,
        out_specs=(anywhere, anywhere),
        scratch_shapes=[
            pltpu.VMEM((tokens, width), bf16),
            pltpu.VMEM((n, tokens, cols), bf16),
            pltpu.VMEM((n, tokens, width), bf16),
            pltpu.VMEM((rows, width), f32),
            pltpu.VMEM((patches, tokens, 2, width), bf16),
            pltpu.VMEM((2, n, per, cols), bf16),
            pltpu.VMEM((n * per + rows, cols), bf16),
            pltpu.VMEM((n * per + rows, cols), bf16),
            pltpu.VMEM((3, width, cols), bf16),
            pltpu.VMEM((n, cols, cols), bf16),
            pltpu.VMEM(norm_gain.shape, f32),
            pltpu.VMEM((3, modulation.shape[1], width), f32),
            pltpu.SMEM(patch_order.shape, jnp.int32),
            pltpu.SMEM(timestep.shape, jnp.int32),
            pltpu.VMEM((n, tokens, 2, cols), bf16),
            pltpu.VMEM((n, rows, cols), bf16),
            pltpu.VMEM((n, tokens, cols), bf16),
            dma((3, parts)),
            dma((n,)),
            dma((7,)),
            dma((parts, n)),
            dma((parts, n)),
        ]
        + [dma((n,))] * 12,
        compiler_params=pltpu.CompilerParams(
            collective_id=0, has_side_effects=True, vmem_limit_bytes=60 * 2**20
        ),
    )(
        patch_order,
        timestep,
        hidden,
        kv_cache,
        jnp.transpose(w_qkv[0], (1, 0, 2)),
        w_out[0].reshape(n, cols, cols),
        norm_gain,
        jnp.transpose(modulation[0], (1, 0, 2)),
    )


def block_step(*arrays):
    hidden, w_qkv, norm_gain = arrays[0], arrays[2], arrays[4]
    lanes = norm_gain.shape[2]
    whole_heads = lanes % 128 == 0 and w_qkv.shape[3] % lanes == 0
    rows, per = lax.axis_size("seq") * hidden.shape[1], arrays[1].shape[1] * hidden.shape[1]
    whole_tiles = rows % 16 == 0 and per % 16 == 0
    if whole_heads and whole_tiles and lax.axis_size("seq") > 1 and lax.axis_size("section") > 1:
        return fused(*arrays)
    return body(*arrays)


def solution(mesh):
    return jax.shard_map(
        block_step,
        mesh=mesh,
        in_specs=(
            P("section", ("groups", "seq"), None),
            P("section", None, ("groups", "seq"), None, None),
            P("section", None, None, "seq"),
            P("section", None, "seq"),
            P("section", None, None),
            P("section", None, None, None),
            P("groups"),
            P("groups"),
        ),
        out_specs=(
            P("section", ("groups", "seq"), None),
            P("section", ("groups", "seq"), None, None),
        ),
        check_vma=False,
    )
```

```python
import functools
import math

import jax
import jax.numpy as jnp
from jax import lax
from jax.experimental import pallas as pl
from jax.experimental.pallas import tpu as pltpu
from jax.sharding import PartitionSpec as P


def passed_along(array, axis, by):
    count = lax.axis_size(axis)
    return lax.ppermute(array, axis, [(i, (i + by) % count) for i in range(count)])


def layer_norm(values_in):
    center = values_in - jnp.mean(values_in, axis=-1, keepdims=True)
    spread = jnp.mean(center * center, axis=-1, keepdims=True)
    return center * lax.rsqrt(spread + 1e-06)


def head_norm(values_in, gain):
    square = jnp.mean(values_in * values_in, axis=-1, keepdims=True)
    return values_in * lax.rsqrt(square + 1e-06) * gain


def body(hidden, kv_cache, w_qkv, w_out, norm_gain, modulation, patch_order, timestep):
    section_index = lax.axis_index("section")
    patch_index = lax.dynamic_index_in_dim(patch_order, section_index, 0, keepdims=False)
    step_index = lax.dynamic_index_in_dim(timestep, section_index, 0, keepdims=False)
    modulate = lax.dynamic_index_in_dim(modulation[0], step_index, 0, keepdims=False)
    model_width = hidden.shape[2]
    head_size = norm_gain.shape[2]
    head_count = model_width // head_size
    col_width = w_qkv.shape[3]
    rows_in = hidden[0].astype(jnp.float32)
    own_count = rows_in.shape[0]
    normed = (layer_norm(rows_in) * (1.0 + modulate[1]) + modulate[0]).astype(jnp.bfloat16)
    w_local = w_qkv[0].reshape(model_width, 3 * col_width)
    projected = jnp.dot(
        lax.all_gather(normed, "seq", axis=0, tiled=True),
        w_local,
        preferred_element_type=jnp.float32,
    ).astype(jnp.bfloat16)
    patch_len = projected.shape[0]
    projected = projected.reshape(patch_len, 3, col_width)
    query_cols = lax.all_gather(projected[:, 0], "seq", axis=1, tiled=True)
    kv_rows = lax.all_to_all(projected[:, 1:], "seq", split_axis=0, concat_axis=2, tiled=True)
    queries = head_norm(
        query_cols.astype(jnp.float32).reshape(patch_len, head_count, head_size), norm_gain[0, 0]
    ).astype(jnp.bfloat16)
    key_rows = head_norm(
        kv_rows[:, 0].astype(jnp.float32).reshape(own_count, head_count, head_size), norm_gain[0, 1]
    ).astype(jnp.bfloat16)
    fresh = jnp.stack([key_rows.reshape(own_count, model_width), kv_rows[:, 1]], axis=1)
    zero = jnp.zeros((), jnp.int32)
    local_kv = lax.dynamic_update_slice(kv_cache[0], fresh[None], (patch_index, zero, zero, zero))
    patch_count = local_kv.shape[0]
    local_keys = local_kv[:, :, 0].reshape(patch_count * own_count, head_count, head_size)
    local_values = local_kv[:, :, 1].reshape(patch_count * own_count, head_count, head_size)
    scores = jnp.einsum(
        "thd,shd->hts", queries, local_keys, preferred_element_type=jnp.float32
    ) / math.sqrt(head_size)
    row_top = lax.pmax(jnp.max(scores, axis=-1), "seq")
    weights = jnp.exp(scores - row_top[:, :, None]).astype(jnp.bfloat16)
    denominator = jnp.sum(weights, axis=-1, dtype=jnp.float32).T
    numerator = jnp.einsum(
        "hts,shd->thd", weights, local_values, preferred_element_type=jnp.float32
    ).reshape(patch_len, model_width)
    totals, counts = (
        lax.psum(numerator.astype(jnp.bfloat16), "seq").astype(jnp.float32),
        lax.psum(denominator.astype(jnp.bfloat16), "seq").astype(jnp.float32),
    )
    attention = (totals.reshape(patch_len, head_count, head_size) / counts[:, :, None]).astype(
        jnp.bfloat16
    )
    attention = attention.reshape(patch_len, model_width)
    out_cols = jnp.dot(attention, w_out[0], preferred_element_type=jnp.float32).astype(jnp.bfloat16)
    out_rows = lax.all_to_all(out_cols, "seq", split_axis=0, concat_axis=1, tiled=True)
    block = (rows_in + modulate[2] * out_rows.astype(jnp.float32)).astype(jnp.bfloat16)
    arrived = passed_along(block, "section", 1)
    return (arrived[None], fresh[None])


MESH = pl.DeviceIdType.MESH


def fused_kernel(
    n, sections, chunk,
    patch_hbm, step_hbm, hidden_hbm, cache_hbm, qkv_hbm, out_hbm, gain_hbm, mod_hbm,
    next_hbm, fresh_hbm,
    own_rows, hid_cols, norm_buf, rows_f32, own_cache, cache_stage, cache_in, all_f32, w_qkv, w_out,
    gain, mod, patch, step_at, fresh_stage, att_buf, block_stage,
    sem_qkv, sem_out, sem_small, norm_s, norm_r, hid_s, hid_r, key_s, key_r, value_s, value_r,
    fresh_s, fresh_r, att_s, att_r, blk_s, blk_r,
):
    f32, bf16 = jnp.float32, jnp.bfloat16
    me = lax.axis_index("seq")
    section = lax.axis_index("section")
    after = lax.rem(section + 1, sections)
    before = lax.rem(section + sections - 1, sections)
    tokens, width = own_rows.shape
    cols = w_qkv.shape[2]
    patches = own_cache.shape[0]
    head = gain.shape[2]
    heads = cols // head
    rows = n * tokens
    kept = patches - 1
    per = kept * tokens
    stale = n * per
    parts = width // chunk

    def cols_of(index):
        return pl.ds(pl.multiple_of(index * cols, head), cols)

    upper = me >= n // 2
    edge = jnp.where(upper, n - 1 - me, me)

    def origin(step):
        index = step - 1 + jnp.where(edge <= step - 1, 1, 0)
        return jnp.where(upper, n - 1 - index, index)

    def peer(step):
        return origin(n - step)

    barrier = pltpu.get_barrier_semaphore()
    for step in range(1, n):
        pl.semaphore_signal(
            barrier, inc=1, device_id={"seq": peer(step)}, device_id_type=MESH
        )
    for index in range(n):
        pl.semaphore_signal(
            barrier, inc=1, device_id={"section": before, "seq": index}, device_id_type=MESH
        )
    small = [
        pltpu.make_async_copy(src, dst, sem_small.at[place])
        for place, (src, dst) in enumerate(
            (
                (hidden_hbm.at[0], own_rows),
                (mod_hbm, mod),
                (step_hbm, step_at),
                (patch_hbm, patch),
                (gain_hbm, gain),
                (cache_hbm.at[0], own_cache),
            )
        )
    ]
    for copy in small:
        copy.start()
    qkv_copies = {}
    for part in range(parts):
        for which in (1, 0, 2):
            span = pl.ds(part * chunk, chunk)
            copy = pltpu.make_async_copy(
                qkv_hbm.at[which, span], w_qkv.at[which, span], sem_qkv.at[which, part]
            )
            copy.start()
            qkv_copies[which, part] = copy

    for copy in small[:3]:
        copy.wait()
    chosen = lax.broadcasted_iota(jnp.int32, (mod.shape[1], 1), 0) == step_at[section]
    shift, scale = (
        jnp.sum(jnp.where(chosen, mod[which], 0.0), axis=0, keepdims=True) for which in range(2)
    )
    rows_in = own_rows[...].astype(f32)
    center = rows_in - jnp.mean(rows_in, axis=-1, keepdims=True)
    spread = jnp.mean(center * center, axis=-1, keepdims=True)
    norm_buf[me] = (center * lax.rsqrt(spread + 1e-06) * (1.0 + scale) + shift).astype(bf16)
    pl.semaphore_wait(barrier, 2 * n - 1)

    sends = []

    def send(src, dst, send_sem, recv_sem, device):
        copy = pltpu.make_async_remote_copy(
            src_ref=src, dst_ref=dst, send_sem=send_sem, recv_sem=recv_sem,
            device_id=device, device_id_type=MESH,
        )
        copy.start()
        sends.append(copy)

    def arrival(dst, send_sem, recv_sem, device):
        pltpu.make_async_remote_copy(
            src_ref=dst, dst_ref=dst, send_sem=send_sem, recv_sem=recv_sem,
            device_id=device, device_id_type=MESH,
        ).wait_recv()

    for part in range(parts):
        piece = norm_buf.at[me, :, pl.ds(part * chunk, chunk)]
        for step in range(1, n):
            send(piece, piece, norm_s.at[part, step], norm_r.at[part, me], {"seq": peer(step)})

    for copy in small[3:]:
        copy.wait()
    held = patch[section]
    for slot in range(kept):
        pair = jnp.where(held <= slot, own_cache[slot + 1], own_cache[slot]).astype(f32)
        for which in range(2):
            split = pair[:, which, :].astype(bf16)
            for index in range(n):
                cache_stage[which, index, slot] = split[:, index * cols : (index + 1) * cols]
    for which, (send_sem, recv_sem) in enumerate(((key_s, key_r), (value_s, value_r))):
        for step in range(1, n):
            send(
                cache_stage.at[which, peer(step)], cache_in.at[which, me],
                send_sem.at[step], recv_sem.at[me], {"seq": peer(step)},
            )
        cache_in[which, me] = cache_stage[which, me]
    for step in range(1, n):
        send(
            own_rows.at[:, cols_of(peer(step))], hid_cols.at[me], hid_s.at[step], hid_r.at[me],
            {"seq": peer(step)},
        )
    hid_cols[me] = own_rows[:, cols_of(me)]
    out_copies = [
        pltpu.make_async_copy(out_hbm.at[index], w_out.at[index], sem_out.at[index])
        for index in range(n)
    ]
    for copy in out_copies:
        copy.start()

    totals = [jnp.zeros((rows, cols), f32)] * 3
    for part in range(parts):
        span = slice(part * chunk, (part + 1) * chunk)
        for step in range(1, n):
            source = origin(step)
            arrival(
                norm_buf.at[source, :, pl.ds(part * chunk, chunk)],
                norm_s.at[part, step], norm_r.at[part, source], {"seq": source},
            )
        for index in range(n):
            rows_f32[index * tokens : (index + 1) * tokens, span] = norm_buf[index, :, span].astype(
                f32
            )
        normed = rows_f32[:, span].astype(bf16)
        for which in (1, 0, 2):
            qkv_copies[which, part].wait()
            totals[which] += jnp.dot(
                normed, w_qkv[which, span, :], preferred_element_type=f32
            )
    projected = [total.astype(bf16) for total in totals]

    def head_norms(projected, which):
        done = []
        for index in range(heads):
            vector = projected[:, index * head : (index + 1) * head].astype(f32)
            square = jnp.mean(vector * vector, axis=-1, keepdims=True)
            normal = vector * lax.rsqrt(square + 1e-06) * gain[0, which : which + 1, :]
            done.append(normal.astype(bf16))
        return done

    def gathered(which, fresh, send_sem, recv_sem):
        for step in range(1, n):
            source = origin(step)
            arrival(
                cache_in.at[which, source], send_sem.at[step], recv_sem.at[source], {"seq": source}
            )
        for index in range(n):
            for slot in range(kept):
                first = index * per + slot * tokens
                all_f32[which, first : first + tokens, :] = cache_in[which, index, slot].astype(f32)
        all_f32[which, stale:, :] = fresh.astype(f32)
        return all_f32[which].astype(bf16)

    fresh_keys = jnp.concatenate(head_norms(projected[1], 1), axis=1)
    queries = head_norms(projected[0], 0)
    keys = gathered(0, fresh_keys, key_s, key_r)
    count = stale + rows
    column = lax.broadcasted_iota(jnp.int32, (1, count), 1)
    group = jnp.where(column < stale, column // per, (column - stale) // tokens)
    row_group = lax.broadcasted_iota(jnp.int32, (n * rows, 1), 0) // rows
    same_group = row_group == group
    weights = []
    for index in range(heads):
        scores = lax.dot_general(
            queries[index], keys[:, index * head : (index + 1) * head],
            (((1,), (1,)), ((), ())), preferred_element_type=f32,
        ) * (1.0 / math.sqrt(head))
        top = jnp.max(scores, axis=-1, keepdims=True)
        weight = jnp.exp(scores - top)
        grouped = jnp.where(same_group, jnp.concatenate([weight] * n, axis=0), 0.0)
        weights.append(grouped.astype(bf16))

    fresh_values = projected[2]
    values = gathered(1, fresh_values, value_s, value_r)
    ones = jnp.ones((count, head), bf16)
    for index in range(heads):
        span = slice(index * head, (index + 1) * head)
        both = jnp.concatenate([values[:, span], ones], axis=1)
        partial = jnp.dot(weights[index], both, preferred_element_type=f32)
        partial = partial.astype(bf16).astype(f32)
        sums = sum(partial[i * rows : (i + 1) * rows] for i in range(n))
        att_buf[me, :, span] = (sums[:, :head] / sums[:, head:]).astype(bf16)
    for step in range(1, n):
        send(att_buf.at[me], att_buf.at[me], att_s.at[step], att_r.at[me], {"seq": peer(step)})

    keys_f32 = fresh_keys.astype(f32)
    values_f32 = fresh_values.astype(f32)
    is_key = lax.broadcasted_iota(jnp.int32, (tokens, 2, cols), 1) == 0
    for index in range(n):
        span = slice(index * tokens, (index + 1) * tokens)
        fresh_stage[index] = jnp.where(
            is_key, keys_f32[span][:, None, :], values_f32[span][:, None, :]
        ).astype(bf16)
    own_fresh = pltpu.make_async_copy(
        fresh_stage.at[me], fresh_hbm.at[0, :, :, cols_of(me)], sem_small.at[6]
    )
    own_fresh.start()
    for step in range(1, n):
        send(
            fresh_stage.at[peer(step)], fresh_hbm.at[0, :, :, cols_of(me)],
            fresh_s.at[step], fresh_r.at[me], {"seq": peer(step)},
        )
    gate = jnp.sum(jnp.where(chosen, mod[2, :, cols_of(me)], 0.0), axis=0, keepdims=True)

    for copy in out_copies:
        copy.wait()
    total = jnp.dot(att_buf[me], w_out[me], preferred_element_type=f32)
    for step in range(1, n):
        source = origin(step)
        arrival(att_buf.at[source], att_s.at[step], att_r.at[source], {"seq": source})
        total += jnp.dot(att_buf[source], w_out[source], preferred_element_type=f32)
    for step in range(1, n):
        source = origin(step)
        arrival(hid_cols.at[source], hid_s.at[step], hid_r.at[source], {"seq": source})
    change = gate * total.astype(bf16).astype(f32)
    for index in range(n):
        block = hid_cols[index].astype(f32) + change[index * tokens : (index + 1) * tokens]
        block_stage[index] = block.astype(bf16)
    for index in range(n):
        send(
            block_stage.at[index], next_hbm.at[0, :, cols_of(me)],
            blk_s.at[index], blk_r.at[me], {"section": after, "seq": index},
        )
    own_fresh.wait()
    for step in range(1, n):
        source = origin(step)
        arrival(
            fresh_hbm.at[0, :, :, cols_of(source)], fresh_s.at[step], fresh_r.at[source],
            {"seq": source},
        )
    for index in range(n):
        arrival(
            next_hbm.at[0, :, cols_of(index)], blk_s.at[index], blk_r.at[index],
            {"section": before, "seq": index},
        )
    for copy in sends:
        copy.wait_send()


def place_kernel(next_ref, fresh_ref, next_out, fresh_out, sems):
    copies = [
        pltpu.make_async_copy(next_ref, next_out, sems.at[0]),
        pltpu.make_async_copy(fresh_ref, fresh_out, sems.at[1]),
    ]
    for copy in copies:
        copy.start()
    for copy in copies:
        copy.wait()


def fused(hidden, kv_cache, w_qkv, w_out, norm_gain, modulation, patch_order, timestep):
    n = lax.axis_size("seq")
    sections = lax.axis_size("section")
    tokens, width = hidden.shape[1:]
    patches = kv_cache.shape[1]
    cols = w_qkv.shape[3]
    rows = n * tokens
    chunk = width // 3 if width % 48 == 0 else width
    parts = width // chunk
    bf16, f32 = jnp.bfloat16, jnp.float32
    anywhere = pl.BlockSpec(memory_space=pl.ANY)
    in_hbm = pl.BlockSpec(memory_space=pltpu.HBM)
    dma = pltpu.SemaphoreType.DMA
    results = pl.pallas_call(
        functools.partial(fused_kernel, n, sections, chunk),
        out_shape=(
            pltpu.VMEM(hidden.shape, bf16),
            pltpu.VMEM((1, tokens, 2, width), bf16),
        ),
        in_specs=[in_hbm] * 8,
        out_specs=(anywhere, anywhere),
        scratch_shapes=[
            pltpu.VMEM((tokens, width), bf16),
            pltpu.VMEM((n, tokens, cols), bf16),
            pltpu.VMEM((n, tokens, width), bf16),
            pltpu.VMEM((rows, width), f32),
            pltpu.VMEM((patches, tokens, 2, width), bf16),
            pltpu.VMEM((2, n, patches - 1, tokens, cols), bf16),
            pltpu.VMEM((2, n, patches - 1, tokens, cols), bf16),
            pltpu.VMEM((2, patches * rows, cols), f32),
            pltpu.VMEM((3, width, cols), bf16),
            pltpu.VMEM((n, cols, cols), bf16),
            pltpu.VMEM(norm_gain.shape, f32),
            pltpu.VMEM((3, modulation.shape[1], width), f32),
            pltpu.SMEM(patch_order.shape, jnp.int32),
            pltpu.SMEM(timestep.shape, jnp.int32),
            pltpu.VMEM((n, tokens, 2, cols), bf16),
            pltpu.VMEM((n, rows, cols), bf16),
            pltpu.VMEM((n, tokens, cols), bf16),
            dma((3, parts)),
            dma((n,)),
            dma((7,)),
            dma((parts, n)),
            dma((parts, n)),
        ]
        + [dma((n,))] * 12,
        compiler_params=pltpu.CompilerParams(
            collective_id=0, has_side_effects=True, vmem_limit_bytes=60 * 2**20
        ),
    )(
        patch_order,
        timestep,
        hidden,
        kv_cache,
        jnp.transpose(w_qkv[0], (1, 0, 2)),
        w_out[0].reshape(n, cols, cols),
        norm_gain,
        jnp.transpose(modulation[0], (1, 0, 2)),
    )
    return pl.pallas_call(
        place_kernel,
        out_shape=tuple(jax.ShapeDtypeStruct(result.shape, bf16) for result in results),
        in_specs=[anywhere] * 2,
        out_specs=(anywhere, anywhere),
        scratch_shapes=[dma((2,))],
    )(*results)


def block_step(*arrays):
    hidden, w_qkv, norm_gain = arrays[0], arrays[2], arrays[4]
    lanes = norm_gain.shape[2]
    whole_heads = lanes % 128 == 0 and w_qkv.shape[3] % lanes == 0
    whole_tiles = lax.axis_size("seq") * hidden.shape[1] % 16 == 0 and arrays[1].shape[1] > 1
    if whole_heads and whole_tiles and lax.axis_size("seq") > 1 and lax.axis_size("section") > 1:
        return fused(*arrays)
    return body(*arrays)


def solution(mesh):
    return jax.shard_map(
        block_step,
        mesh=mesh,
        in_specs=(
            P("section", ("groups", "seq"), None),
            P("section", None, ("groups", "seq"), None, None),
            P("section", None, None, "seq"),
            P("section", None, "seq"),
            P("section", None, None),
            P("section", None, None, None),
            P("groups"),
            P("groups"),
        ),
        out_specs=(
            P("section", ("groups", "seq"), None),
            P("section", ("groups", "seq"), None, None),
        ),
        check_vma=False,
    )
```

```python
import functools
import math

import jax
import jax.numpy as jnp
from jax import lax
from jax.experimental import pallas as pl
from jax.experimental.pallas import tpu as pltpu
from jax.sharding import PartitionSpec as P


def passed_along(array, axis, by):
    count = lax.axis_size(axis)
    return lax.ppermute(array, axis, [(i, (i + by) % count) for i in range(count)])


def layer_norm(values_in):
    center = values_in - jnp.mean(values_in, axis=-1, keepdims=True)
    spread = jnp.mean(center * center, axis=-1, keepdims=True)
    return center * lax.rsqrt(spread + 1e-06)


def head_norm(values_in, gain):
    square = jnp.mean(values_in * values_in, axis=-1, keepdims=True)
    return values_in * lax.rsqrt(square + 1e-06) * gain


def body(hidden, kv_cache, w_qkv, w_out, norm_gain, modulation, patch_order, timestep):
    section_index = lax.axis_index("section")
    patch_index = lax.dynamic_index_in_dim(patch_order, section_index, 0, keepdims=False)
    step_index = lax.dynamic_index_in_dim(timestep, section_index, 0, keepdims=False)
    modulate = lax.dynamic_index_in_dim(modulation[0], step_index, 0, keepdims=False)
    model_width = hidden.shape[2]
    head_size = norm_gain.shape[2]
    head_count = model_width // head_size
    col_width = w_qkv.shape[3]
    rows_in = hidden[0].astype(jnp.float32)
    own_count = rows_in.shape[0]
    normed = (layer_norm(rows_in) * (1.0 + modulate[1]) + modulate[0]).astype(jnp.bfloat16)
    w_local = w_qkv[0].reshape(model_width, 3 * col_width)
    projected = jnp.dot(
        lax.all_gather(normed, "seq", axis=0, tiled=True),
        w_local,
        preferred_element_type=jnp.float32,
    ).astype(jnp.bfloat16)
    patch_len = projected.shape[0]
    projected = projected.reshape(patch_len, 3, col_width)
    query_cols = lax.all_gather(projected[:, 0], "seq", axis=1, tiled=True)
    kv_rows = lax.all_to_all(projected[:, 1:], "seq", split_axis=0, concat_axis=2, tiled=True)
    queries = head_norm(
        query_cols.astype(jnp.float32).reshape(patch_len, head_count, head_size), norm_gain[0, 0]
    ).astype(jnp.bfloat16)
    key_rows = head_norm(
        kv_rows[:, 0].astype(jnp.float32).reshape(own_count, head_count, head_size), norm_gain[0, 1]
    ).astype(jnp.bfloat16)
    fresh = jnp.stack([key_rows.reshape(own_count, model_width), kv_rows[:, 1]], axis=1)
    zero = jnp.zeros((), jnp.int32)
    local_kv = lax.dynamic_update_slice(kv_cache[0], fresh[None], (patch_index, zero, zero, zero))
    patch_count = local_kv.shape[0]
    local_keys = local_kv[:, :, 0].reshape(patch_count * own_count, head_count, head_size)
    local_values = local_kv[:, :, 1].reshape(patch_count * own_count, head_count, head_size)
    scores = jnp.einsum(
        "thd,shd->hts", queries, local_keys, preferred_element_type=jnp.float32
    ) / math.sqrt(head_size)
    row_top = lax.pmax(jnp.max(scores, axis=-1), "seq")
    weights = jnp.exp(scores - row_top[:, :, None]).astype(jnp.bfloat16)
    denominator = jnp.sum(weights, axis=-1, dtype=jnp.float32).T
    numerator = jnp.einsum(
        "hts,shd->thd", weights, local_values, preferred_element_type=jnp.float32
    ).reshape(patch_len, model_width)
    totals, counts = (
        lax.psum(numerator.astype(jnp.bfloat16), "seq").astype(jnp.float32),
        lax.psum(denominator.astype(jnp.bfloat16), "seq").astype(jnp.float32),
    )
    attention = (totals.reshape(patch_len, head_count, head_size) / counts[:, :, None]).astype(
        jnp.bfloat16
    )
    attention = attention.reshape(patch_len, model_width)
    out_cols = jnp.dot(attention, w_out[0], preferred_element_type=jnp.float32).astype(jnp.bfloat16)
    out_rows = lax.all_to_all(out_cols, "seq", split_axis=0, concat_axis=1, tiled=True)
    block = (rows_in + modulate[2] * out_rows.astype(jnp.float32)).astype(jnp.bfloat16)
    arrived = passed_along(block, "section", 1)
    return (arrived[None], fresh[None])


MESH = pl.DeviceIdType.MESH


def fused_kernel(
    n, sections, chunk,
    patch_hbm, step_hbm, hidden_hbm, cache_hbm, qkv_hbm, out_hbm, gain_hbm, mod_hbm,
    next_hbm, fresh_hbm,
    own_rows, hid_cols, norm_buf, rows_f32, own_cache, cache_stage, cache_in, all_f32, w_qkv, w_out,
    gain, mod, patch, step_at, fresh_stage, att_buf, block_stage,
    sem_qkv, sem_out, sem_small, norm_s, norm_r, hid_s, hid_r, key_s, key_r, value_s, value_r,
    fresh_s, fresh_r, att_s, att_r, blk_s, blk_r,
):
    f32, bf16 = jnp.float32, jnp.bfloat16
    me = lax.axis_index("seq")
    section = lax.axis_index("section")
    after = lax.rem(section + 1, sections)
    before = lax.rem(section + sections - 1, sections)
    tokens, width = own_rows.shape
    cols = w_qkv.shape[2]
    patches = own_cache.shape[0]
    head = gain.shape[2]
    heads = cols // head
    rows = n * tokens
    kept = patches - 1
    per = kept * tokens
    stale = n * per
    parts = width // chunk

    def cols_of(index):
        return pl.ds(pl.multiple_of(index * cols, head), cols)

    upper = me >= n // 2
    edge = jnp.where(upper, n - 1 - me, me)

    def origin(step):
        index = step - 1 + jnp.where(edge <= step - 1, 1, 0)
        return jnp.where(upper, n - 1 - index, index)

    def peer(step):
        return origin(n - step)

    barrier = pltpu.get_barrier_semaphore()
    for step in range(1, n):
        pl.semaphore_signal(
            barrier, inc=1, device_id={"seq": peer(step)}, device_id_type=MESH
        )
    for index in range(n):
        pl.semaphore_signal(
            barrier, inc=1, device_id={"section": before, "seq": index}, device_id_type=MESH
        )
    small = [
        pltpu.make_async_copy(src, dst, sem_small.at[place])
        for place, (src, dst) in enumerate(
            (
                (hidden_hbm.at[0], own_rows),
                (mod_hbm, mod),
                (step_hbm, step_at),
                (patch_hbm, patch),
                (gain_hbm, gain),
                (cache_hbm.at[0], own_cache),
            )
        )
    ]
    for copy in small:
        copy.start()
    qkv_copies = {}
    for part in range(parts):
        for which in (1, 0, 2):
            span = pl.ds(part * chunk, chunk)
            copy = pltpu.make_async_copy(
                qkv_hbm.at[which, span], w_qkv.at[which, span], sem_qkv.at[which, part]
            )
            qkv_copies[which, part] = copy
            if part == 0:
                copy.start()

    for copy in small[:3]:
        copy.wait()
    chosen = lax.broadcasted_iota(jnp.int32, (mod.shape[1], 1), 0) == step_at[section]
    shift, scale = (
        jnp.sum(jnp.where(chosen, mod[which], 0.0), axis=0, keepdims=True) for which in range(2)
    )
    rows_in = own_rows[...].astype(f32)
    center = rows_in - jnp.mean(rows_in, axis=-1, keepdims=True)
    spread = jnp.mean(center * center, axis=-1, keepdims=True)
    norm_buf[me] = (center * lax.rsqrt(spread + 1e-06) * (1.0 + scale) + shift).astype(bf16)
    pl.semaphore_wait(barrier, 2 * n - 1)

    sends = []

    def send(src, dst, send_sem, recv_sem, device):
        copy = pltpu.make_async_remote_copy(
            src_ref=src, dst_ref=dst, send_sem=send_sem, recv_sem=recv_sem,
            device_id=device, device_id_type=MESH,
        )
        copy.start()
        sends.append(copy)

    def arrival(dst, send_sem, recv_sem, device):
        pltpu.make_async_remote_copy(
            src_ref=dst, dst_ref=dst, send_sem=send_sem, recv_sem=recv_sem,
            device_id=device, device_id_type=MESH,
        ).wait_recv()

    for part in range(parts):
        piece = norm_buf.at[me, :, pl.ds(part * chunk, chunk)]
        for step in range(1, n):
            send(piece, piece, norm_s.at[part, step], norm_r.at[part, me], {"seq": peer(step)})

    for (which, part), copy in qkv_copies.items():
        if part > 0:
            copy.start()

    for copy in small[3:]:
        copy.wait()
    held = patch[section]
    for slot in range(kept):
        pair = jnp.where(held <= slot, own_cache[slot + 1], own_cache[slot]).astype(f32)
        for which in range(2):
            split = pair[:, which, :].astype(bf16)
            for index in range(n):
                cache_stage[which, index, slot] = split[:, index * cols : (index + 1) * cols]
    for which, (send_sem, recv_sem) in enumerate(((key_s, key_r), (value_s, value_r))):
        for step in range(1, n):
            send(
                cache_stage.at[which, peer(step)], cache_in.at[which, me],
                send_sem.at[step], recv_sem.at[me], {"seq": peer(step)},
            )
        cache_in[which, me] = cache_stage[which, me]
    for step in range(1, n):
        send(
            own_rows.at[:, cols_of(peer(step))], hid_cols.at[me], hid_s.at[step], hid_r.at[me],
            {"seq": peer(step)},
        )
    hid_cols[me] = own_rows[:, cols_of(me)]
    out_copies = [
        pltpu.make_async_copy(out_hbm.at[index], w_out.at[index], sem_out.at[index])
        for index in range(n)
    ]
    for copy in out_copies:
        copy.start()

    totals = [jnp.zeros((rows, cols), f32)] * 3
    for part in range(parts):
        span = slice(part * chunk, (part + 1) * chunk)
        for step in range(1, n):
            source = origin(step)
            arrival(
                norm_buf.at[source, :, pl.ds(part * chunk, chunk)],
                norm_s.at[part, step], norm_r.at[part, source], {"seq": source},
            )
        for index in range(n):
            rows_f32[index * tokens : (index + 1) * tokens, span] = norm_buf[index, :, span].astype(
                f32
            )
        normed = rows_f32[:, span].astype(bf16)
        for which in (1, 0, 2):
            qkv_copies[which, part].wait()
            totals[which] += jnp.dot(
                normed, w_qkv[which, span, :], preferred_element_type=f32
            )
    projected = [total.astype(bf16) for total in totals]

    def head_norms(projected, which):
        done = []
        for index in range(heads):
            vector = projected[:, index * head : (index + 1) * head].astype(f32)
            square = jnp.mean(vector * vector, axis=-1, keepdims=True)
            normal = vector * lax.rsqrt(square + 1e-06) * gain[0, which : which + 1, :]
            done.append(normal.astype(bf16))
        return done

    def gathered(which, fresh, send_sem, recv_sem):
        for step in range(1, n):
            source = origin(step)
            arrival(
                cache_in.at[which, source], send_sem.at[step], recv_sem.at[source], {"seq": source}
            )
        for index in range(n):
            for slot in range(kept):
                first = index * per + slot * tokens
                all_f32[which, first : first + tokens, :] = cache_in[which, index, slot].astype(f32)
        all_f32[which, stale:, :] = fresh.astype(f32)
        return all_f32[which].astype(bf16)

    fresh_keys = jnp.concatenate(head_norms(projected[1], 1), axis=1)
    queries = head_norms(projected[0], 0)
    keys = gathered(0, fresh_keys, key_s, key_r)
    count = stale + rows
    column = lax.broadcasted_iota(jnp.int32, (1, count), 1)
    group = jnp.where(column < stale, column // per, (column - stale) // tokens)
    row_group = lax.broadcasted_iota(jnp.int32, (n * rows, 1), 0) // rows
    same_group = row_group == group
    weights = []
    for index in range(heads):
        scores = lax.dot_general(
            queries[index], keys[:, index * head : (index + 1) * head],
            (((1,), (1,)), ((), ())), preferred_element_type=f32,
        ) * (1.0 / math.sqrt(head))
        top = jnp.max(scores, axis=-1, keepdims=True)
        weight = jnp.exp(scores - top)
        grouped = jnp.where(same_group, jnp.concatenate([weight] * n, axis=0), 0.0)
        weights.append(grouped.astype(bf16))

    fresh_values = projected[2]
    keys_f32 = fresh_keys.astype(f32)
    values_f32 = fresh_values.astype(f32)
    is_key = lax.broadcasted_iota(jnp.int32, (tokens, 2, cols), 1) == 0
    for index in range(n):
        span = slice(index * tokens, (index + 1) * tokens)
        fresh_stage[index] = jnp.where(
            is_key, keys_f32[span][:, None, :], values_f32[span][:, None, :]
        ).astype(bf16)
    own_fresh = pltpu.make_async_copy(
        fresh_stage.at[me], fresh_hbm.at[0, :, :, cols_of(me)], sem_small.at[6]
    )
    own_fresh.start()
    for step in range(1, n):
        send(
            fresh_stage.at[peer(step)], fresh_hbm.at[0, :, :, cols_of(me)],
            fresh_s.at[step], fresh_r.at[me], {"seq": peer(step)},
        )
    values = gathered(1, fresh_values, value_s, value_r)
    ones = jnp.ones((count, head), bf16)
    for index in range(heads):
        span = slice(index * head, (index + 1) * head)
        both = jnp.concatenate([values[:, span], ones], axis=1)
        partial = jnp.dot(weights[index], both, preferred_element_type=f32)
        partial = partial.astype(bf16).astype(f32)
        sums = sum(partial[i * rows : (i + 1) * rows] for i in range(n))
        att_buf[me, :, span] = (sums[:, :head] / sums[:, head:]).astype(bf16)
    for step in range(1, n):
        send(att_buf.at[me], att_buf.at[me], att_s.at[step], att_r.at[me], {"seq": peer(step)})

    gate = jnp.sum(jnp.where(chosen, mod[2, :, cols_of(me)], 0.0), axis=0, keepdims=True)

    for copy in out_copies:
        copy.wait()
    total = jnp.dot(att_buf[me], w_out[me], preferred_element_type=f32)
    for step in range(1, n):
        source = origin(step)
        arrival(att_buf.at[source], att_s.at[step], att_r.at[source], {"seq": source})
        total += jnp.dot(att_buf[source], w_out[source], preferred_element_type=f32)
    for step in range(1, n):
        source = origin(step)
        arrival(hid_cols.at[source], hid_s.at[step], hid_r.at[source], {"seq": source})
    change = gate * total.astype(bf16).astype(f32)
    for index in range(n):
        block = hid_cols[index].astype(f32) + change[index * tokens : (index + 1) * tokens]
        block_stage[index] = block.astype(bf16)
    for index in range(n):
        send(
            block_stage.at[index], next_hbm.at[0, :, cols_of(me)],
            blk_s.at[index], blk_r.at[me], {"section": after, "seq": index},
        )
    own_fresh.wait()
    for step in range(1, n):
        source = origin(step)
        arrival(
            fresh_hbm.at[0, :, :, cols_of(source)], fresh_s.at[step], fresh_r.at[source],
            {"seq": source},
        )
    for index in range(n):
        arrival(
            next_hbm.at[0, :, cols_of(index)], blk_s.at[index], blk_r.at[index],
            {"section": before, "seq": index},
        )
    for copy in sends:
        copy.wait_send()


def fused(hidden, kv_cache, w_qkv, w_out, norm_gain, modulation, patch_order, timestep):
    n = lax.axis_size("seq")
    sections = lax.axis_size("section")
    tokens, width = hidden.shape[1:]
    patches = kv_cache.shape[1]
    cols = w_qkv.shape[3]
    rows = n * tokens
    chunk = width // 3 if width % 48 == 0 else width
    parts = width // chunk
    bf16, f32 = jnp.bfloat16, jnp.float32
    anywhere = pl.BlockSpec(memory_space=pl.ANY)
    in_hbm = pl.BlockSpec(memory_space=pltpu.HBM)
    dma = pltpu.SemaphoreType.DMA
    return pl.pallas_call(
        functools.partial(fused_kernel, n, sections, chunk),
        out_shape=(
            pltpu.VMEM(hidden.shape, bf16),
            pltpu.VMEM((1, tokens, 2, width), bf16),
        ),
        in_specs=[in_hbm] * 8,
        out_specs=(anywhere, anywhere),
        scratch_shapes=[
            pltpu.VMEM((tokens, width), bf16),
            pltpu.VMEM((n, tokens, cols), bf16),
            pltpu.VMEM((n, tokens, width), bf16),
            pltpu.VMEM((rows, width), f32),
            pltpu.VMEM((patches, tokens, 2, width), bf16),
            pltpu.VMEM((2, n, patches - 1, tokens, cols), bf16),
            pltpu.VMEM((2, n, patches - 1, tokens, cols), bf16),
            pltpu.VMEM((2, patches * rows, cols), f32),
            pltpu.VMEM((3, width, cols), bf16),
            pltpu.VMEM((n, cols, cols), bf16),
            pltpu.VMEM(norm_gain.shape, f32),
            pltpu.VMEM((3, modulation.shape[1], width), f32),
            pltpu.SMEM(patch_order.shape, jnp.int32),
            pltpu.SMEM(timestep.shape, jnp.int32),
            pltpu.VMEM((n, tokens, 2, cols), bf16),
            pltpu.VMEM((n, rows, cols), bf16),
            pltpu.VMEM((n, tokens, cols), bf16),
            dma((3, parts)),
            dma((n,)),
            dma((7,)),
            dma((parts, n)),
            dma((parts, n)),
        ]
        + [dma((n,))] * 12,
        compiler_params=pltpu.CompilerParams(
            collective_id=0, has_side_effects=True, vmem_limit_bytes=60 * 2**20
        ),
    )(
        patch_order,
        timestep,
        hidden,
        kv_cache,
        jnp.transpose(w_qkv[0], (1, 0, 2)),
        w_out[0].reshape(n, cols, cols),
        norm_gain,
        jnp.transpose(modulation[0], (1, 0, 2)),
    )


def block_step(*arrays):
    hidden, w_qkv, norm_gain = arrays[0], arrays[2], arrays[4]
    lanes = norm_gain.shape[2]
    whole_heads = lanes % 128 == 0 and w_qkv.shape[3] % lanes == 0
    whole_tiles = lax.axis_size("seq") * hidden.shape[1] % 16 == 0 and arrays[1].shape[1] > 1
    if whole_heads and whole_tiles and lax.axis_size("seq") > 1 and lax.axis_size("section") > 1:
        return fused(*arrays)
    return body(*arrays)


def solution(mesh):
    return jax.shard_map(
        block_step,
        mesh=mesh,
        in_specs=(
            P("section", ("groups", "seq"), None),
            P("section", None, ("groups", "seq"), None, None),
            P("section", None, None, "seq"),
            P("section", None, "seq"),
            P("section", None, None),
            P("section", None, None, None),
            P("groups"),
            P("groups"),
        ),
        out_specs=(
            P("section", ("groups", "seq"), None),
            P("section", ("groups", "seq"), None, None),
        ),
        check_vma=False,
    )
```

```python
import functools
import math

import jax
import jax.numpy as jnp
from jax import lax
from jax.experimental import pallas as pl
from jax.experimental.pallas import tpu as pltpu
from jax.sharding import PartitionSpec as P


def passed_along(array, axis, by):
    count = lax.axis_size(axis)
    return lax.ppermute(array, axis, [(i, (i + by) % count) for i in range(count)])


def layer_norm(values_in):
    center = values_in - jnp.mean(values_in, axis=-1, keepdims=True)
    spread = jnp.mean(center * center, axis=-1, keepdims=True)
    return center * lax.rsqrt(spread + 1e-06)


def head_norm(values_in, gain):
    square = jnp.mean(values_in * values_in, axis=-1, keepdims=True)
    return values_in * lax.rsqrt(square + 1e-06) * gain


def body(hidden, kv_cache, w_qkv, w_out, norm_gain, modulation, patch_order, timestep):
    section_index = lax.axis_index("section")
    patch_index = lax.dynamic_index_in_dim(patch_order, section_index, 0, keepdims=False)
    step_index = lax.dynamic_index_in_dim(timestep, section_index, 0, keepdims=False)
    modulate = lax.dynamic_index_in_dim(modulation[0], step_index, 0, keepdims=False)
    model_width = hidden.shape[2]
    head_size = norm_gain.shape[2]
    head_count = model_width // head_size
    col_width = w_qkv.shape[3]
    rows_in = hidden[0].astype(jnp.float32)
    own_count = rows_in.shape[0]
    normed = (layer_norm(rows_in) * (1.0 + modulate[1]) + modulate[0]).astype(jnp.bfloat16)
    w_local = w_qkv[0].reshape(model_width, 3 * col_width)
    projected = jnp.dot(
        lax.all_gather(normed, "seq", axis=0, tiled=True),
        w_local,
        preferred_element_type=jnp.float32,
    ).astype(jnp.bfloat16)
    patch_len = projected.shape[0]
    projected = projected.reshape(patch_len, 3, col_width)
    query_cols = lax.all_gather(projected[:, 0], "seq", axis=1, tiled=True)
    kv_rows = lax.all_to_all(projected[:, 1:], "seq", split_axis=0, concat_axis=2, tiled=True)
    queries = head_norm(
        query_cols.astype(jnp.float32).reshape(patch_len, head_count, head_size), norm_gain[0, 0]
    ).astype(jnp.bfloat16)
    key_rows = head_norm(
        kv_rows[:, 0].astype(jnp.float32).reshape(own_count, head_count, head_size), norm_gain[0, 1]
    ).astype(jnp.bfloat16)
    fresh = jnp.stack([key_rows.reshape(own_count, model_width), kv_rows[:, 1]], axis=1)
    zero = jnp.zeros((), jnp.int32)
    local_kv = lax.dynamic_update_slice(kv_cache[0], fresh[None], (patch_index, zero, zero, zero))
    patch_count = local_kv.shape[0]
    local_keys = local_kv[:, :, 0].reshape(patch_count * own_count, head_count, head_size)
    local_values = local_kv[:, :, 1].reshape(patch_count * own_count, head_count, head_size)
    scores = jnp.einsum(
        "thd,shd->hts", queries, local_keys, preferred_element_type=jnp.float32
    ) / math.sqrt(head_size)
    row_top = lax.pmax(jnp.max(scores, axis=-1), "seq")
    weights = jnp.exp(scores - row_top[:, :, None]).astype(jnp.bfloat16)
    denominator = jnp.sum(weights, axis=-1, dtype=jnp.float32).T
    numerator = jnp.einsum(
        "hts,shd->thd", weights, local_values, preferred_element_type=jnp.float32
    ).reshape(patch_len, model_width)
    totals, counts = (
        lax.psum(numerator.astype(jnp.bfloat16), "seq").astype(jnp.float32),
        lax.psum(denominator.astype(jnp.bfloat16), "seq").astype(jnp.float32),
    )
    attention = (totals.reshape(patch_len, head_count, head_size) / counts[:, :, None]).astype(
        jnp.bfloat16
    )
    attention = attention.reshape(patch_len, model_width)
    out_cols = jnp.dot(attention, w_out[0], preferred_element_type=jnp.float32).astype(jnp.bfloat16)
    out_rows = lax.all_to_all(out_cols, "seq", split_axis=0, concat_axis=1, tiled=True)
    block = (rows_in + modulate[2] * out_rows.astype(jnp.float32)).astype(jnp.bfloat16)
    arrived = passed_along(block, "section", 1)
    return (arrived[None], fresh[None])


MESH = pl.DeviceIdType.MESH


def fused_kernel(
    n, sections, chunk, cuts,
    patch_hbm, step_hbm, hidden_hbm, cache_hbm, qkv_hbm, out_hbm, gain_hbm, mod_hbm,
    next_hbm, fresh_hbm,
    own_rows, hid_cols, norm_buf, rows_f32, own_cache, cache_stage, cache_in, all_f32, w_qkv, w_out,
    gain, mod, patch, step_at, fresh_stage, att_buf, block_stage,
    sem_qkv, sem_out, sem_small, norm_s, norm_r, hid_s, hid_r, key_s, key_r, value_s, value_r,
    fresh_s, fresh_r, att_s, att_r, blk_s, blk_r,
):
    f32, bf16 = jnp.float32, jnp.bfloat16
    me = lax.axis_index("seq")
    section = lax.axis_index("section")
    after = lax.rem(section + 1, sections)
    before = lax.rem(section + sections - 1, sections)
    tokens, width = own_rows.shape
    cols = w_qkv.shape[2]
    patches = own_cache.shape[0]
    head = gain.shape[2]
    heads = cols // head
    rows = n * tokens
    kept = patches - 1
    per = kept * tokens
    stale = n * per
    parts = width // chunk

    def cols_of(index):
        return pl.ds(pl.multiple_of(index * cols, head), cols)

    upper = me >= n // 2
    edge = jnp.where(upper, n - 1 - me, me)

    def origin(step):
        index = step - 1 + jnp.where(edge <= step - 1, 1, 0)
        return jnp.where(upper, n - 1 - index, index)

    def peer(step):
        return origin(n - step)

    barrier = pltpu.get_barrier_semaphore()
    for step in range(1, n):
        pl.semaphore_signal(
            barrier, inc=1, device_id={"seq": peer(step)}, device_id_type=MESH
        )
    for index in range(n):
        pl.semaphore_signal(
            barrier, inc=1, device_id={"section": before, "seq": index}, device_id_type=MESH
        )
    small = [
        pltpu.make_async_copy(src, dst, sem_small.at[place])
        for place, (src, dst) in enumerate(
            (
                (hidden_hbm.at[0], own_rows),
                (mod_hbm, mod),
                (step_hbm, step_at),
                (patch_hbm, patch),
                (gain_hbm, gain),
                (cache_hbm.at[0], own_cache),
            )
        )
    ]
    for copy in small:
        copy.start()
    qkv_copies = {}
    for part in range(parts):
        for which in (1, 0, 2):
            span = pl.ds(part * chunk, chunk)
            copy = pltpu.make_async_copy(
                qkv_hbm.at[which, span], w_qkv.at[which, span], sem_qkv.at[which, part]
            )
            qkv_copies[which, part] = copy
            if part == 0:
                copy.start()

    for copy in small[:3]:
        copy.wait()
    chosen = lax.broadcasted_iota(jnp.int32, (mod.shape[1], 1), 0) == step_at[section]
    shift, scale = (
        jnp.sum(jnp.where(chosen, mod[which], 0.0), axis=0, keepdims=True) for which in range(2)
    )
    rows_in = own_rows[...].astype(f32)
    center = rows_in - jnp.mean(rows_in, axis=-1, keepdims=True)
    spread = jnp.mean(center * center, axis=-1, keepdims=True)
    norm_buf[me] = (center * lax.rsqrt(spread + 1e-06) * (1.0 + scale) + shift).astype(bf16)
    pl.semaphore_wait(barrier, 2 * n - 1)

    sends = []

    def send(src, dst, send_sem, recv_sem, device):
        copy = pltpu.make_async_remote_copy(
            src_ref=src, dst_ref=dst, send_sem=send_sem, recv_sem=recv_sem,
            device_id=device, device_id_type=MESH,
        )
        copy.start()
        sends.append(copy)

    def arrival(dst, send_sem, recv_sem, device):
        pltpu.make_async_remote_copy(
            src_ref=dst, dst_ref=dst, send_sem=send_sem, recv_sem=recv_sem,
            device_id=device, device_id_type=MESH,
        ).wait_recv()

    for part in range(parts):
        piece = norm_buf.at[me, :, pl.ds(part * chunk, chunk)]
        for step in range(1, n):
            send(piece, piece, norm_s.at[part, step], norm_r.at[part, me], {"seq": peer(step)})

    for (which, part), copy in qkv_copies.items():
        if part > 0:
            copy.start()

    for copy in small[3:]:
        copy.wait()
    held = patch[section]
    for slot in range(kept):
        pair = jnp.where(held <= slot, own_cache[slot + 1], own_cache[slot]).astype(f32)
        for which in range(2):
            split = pair[:, which, :].astype(bf16)
            for index in range(n):
                cache_stage[which, index, slot] = split[:, index * cols : (index + 1) * cols]
    for which, (send_sem, recv_sem) in enumerate(((key_s, key_r), (value_s, value_r))):
        for step in range(1, n):
            send(
                cache_stage.at[which, peer(step)], cache_in.at[which, me],
                send_sem.at[step], recv_sem.at[me], {"seq": peer(step)},
            )
        cache_in[which, me] = cache_stage[which, me]
    for step in range(1, n):
        send(
            own_rows.at[:, cols_of(peer(step))], hid_cols.at[me], hid_s.at[step], hid_r.at[me],
            {"seq": peer(step)},
        )
    hid_cols[me] = own_rows[:, cols_of(me)]
    out_copies = [
        pltpu.make_async_copy(out_hbm.at[index], w_out.at[index], sem_out.at[index])
        for index in range(n)
    ]
    for copy in out_copies:
        copy.start()

    totals = [jnp.zeros((rows, cuts[0][1]), f32)] * 3
    for part in range(parts):
        span = slice(part * chunk, (part + 1) * chunk)
        for step in range(1, n):
            source = origin(step)
            arrival(
                norm_buf.at[source, :, pl.ds(part * chunk, chunk)],
                norm_s.at[part, step], norm_r.at[part, source], {"seq": source},
            )
        for index in range(n):
            rows_f32[index * tokens : (index + 1) * tokens, span] = norm_buf[index, :, span].astype(
                f32
            )
        normed = rows_f32[:, span].astype(bf16)
        for which in (1, 0, 2):
            qkv_copies[which, part].wait()
            totals[which] += jnp.dot(
                normed, w_qkv[which, span, : cuts[0][1]], preferred_element_type=f32
            )
    normed = rows_f32[...].astype(bf16)
    projected = [[total.astype(bf16) for total in totals]]

    def arrivals(which, send_sem, recv_sem):
        for step in range(1, n):
            source = origin(step)
            arrival(
                cache_in.at[which, source], send_sem.at[step], recv_sem.at[source], {"seq": source}
            )
        for index in range(n):
            for slot in range(kept):
                first = index * per + slot * tokens
                all_f32[which, first : first + tokens, :] = cache_in[which, index, slot].astype(f32)

    def head_norms(projected, which):
        done = []
        for index in range(projected.shape[1] // head):
            vector = projected[:, index * head : (index + 1) * head].astype(f32)
            square = jnp.mean(vector * vector, axis=-1, keepdims=True)
            normal = vector * lax.rsqrt(square + 1e-06) * gain[0, which : which + 1, :]
            done.append(normal.astype(bf16))
        return done

    count = stale + rows
    column = lax.broadcasted_iota(jnp.int32, (1, count), 1)
    group = jnp.where(column < stale, column // per, (column - stale) // tokens)
    row_group = lax.broadcasted_iota(jnp.int32, (n * rows, 1), 0) // rows
    same_group = row_group == group
    ones = jnp.ones((count, head), bf16)

    def prepare(projected, first):
        fresh = jnp.concatenate(head_norms(projected[1], 1), axis=1)
        span = slice(first, first + fresh.shape[1])
        all_f32[0, stale:, span] = fresh.astype(f32)
        all_f32[1, stale:, span] = projected[2].astype(f32)
        return head_norms(projected[0], 0)

    def weigh(queries, first):
        weights = []
        for index, query in enumerate(queries):
            span = slice(first + index * head, first + (index + 1) * head)
            scores = lax.dot_general(
                query, all_f32[0, :, span].astype(bf16),
                (((1,), (1,)), ((), ())), preferred_element_type=f32,
            ) * (1.0 / math.sqrt(head))
            top = jnp.max(scores, axis=-1, keepdims=True)
            weight = jnp.exp(scores - top)
            grouped = jnp.where(same_group, jnp.concatenate([weight] * n, axis=0), 0.0)
            weights.append(grouped.astype(bf16))
        return weights

    arrivals(0, key_s, key_r)
    for first, last in cuts[1:]:
        projected.append(
            [
                jnp.dot(normed, w_qkv[which, :, first:last], preferred_element_type=f32).astype(bf16)
                for which in range(3)
            ]
        )
    queries = [prepare(part, first) for (first, _), part in zip(cuts, projected)]
    weights = weigh(queries[0], 0)

    is_key = lax.broadcasted_iota(jnp.int32, (tokens, 2, cols), 1) == 0
    for index in range(n):
        span = slice(stale + index * tokens, stale + (index + 1) * tokens)
        fresh_stage[index] = jnp.where(
            is_key, all_f32[0, span, :][:, None, :], all_f32[1, span, :][:, None, :]
        ).astype(bf16)
    own_fresh = pltpu.make_async_copy(
        fresh_stage.at[me], fresh_hbm.at[0, :, :, cols_of(me)], sem_small.at[6]
    )
    own_fresh.start()
    for step in range(1, n):
        send(
            fresh_stage.at[peer(step)], fresh_hbm.at[0, :, :, cols_of(me)],
            fresh_s.at[step], fresh_r.at[me], {"seq": peer(step)},
        )
    arrivals(1, value_s, value_r)
    for place, (first, last) in enumerate(cuts):
        if place > 0:
            weights += weigh(queries[place], first)
        for index in range(first // head, last // head):
            span = slice(index * head, (index + 1) * head)
            both = jnp.concatenate([all_f32[1, :, span].astype(bf16), ones], axis=1)
            partial = jnp.dot(weights[index], both, preferred_element_type=f32)
            partial = partial.astype(bf16).astype(f32)
            sums = sum(partial[i * rows : (i + 1) * rows] for i in range(n))
            att_buf[me, :, span] = (sums[:, :head] / sums[:, head:]).astype(bf16)
        piece = att_buf.at[me, :, pl.ds(first, last - first)]
        for step in range(1, n):
            send(piece, piece, att_s.at[place, step], att_r.at[place, me], {"seq": peer(step)})

    gate = jnp.sum(jnp.where(chosen, mod[2, :, cols_of(me)], 0.0), axis=0, keepdims=True)

    for copy in out_copies:
        copy.wait()
    total = jnp.dot(att_buf[me], w_out[me], preferred_element_type=f32)
    for place, (first, last) in enumerate(cuts):
        for step in range(1, n):
            source = origin(step)
            arrival(
                att_buf.at[source, :, pl.ds(first, last - first)],
                att_s.at[place, step], att_r.at[place, source], {"seq": source},
            )
            total += jnp.dot(
                att_buf[source, :, first:last], w_out[source, first:last, :],
                preferred_element_type=f32,
            )
    for step in range(1, n):
        source = origin(step)
        arrival(hid_cols.at[source], hid_s.at[step], hid_r.at[source], {"seq": source})
    change = gate * total.astype(bf16).astype(f32)
    for index in range(n):
        block = hid_cols[index].astype(f32) + change[index * tokens : (index + 1) * tokens]
        block_stage[index] = block.astype(bf16)
    for index in range(n):
        send(
            block_stage.at[index], next_hbm.at[0, :, cols_of(me)],
            blk_s.at[index], blk_r.at[me], {"section": after, "seq": index},
        )
    own_fresh.wait()
    for step in range(1, n):
        source = origin(step)
        arrival(
            fresh_hbm.at[0, :, :, cols_of(source)], fresh_s.at[step], fresh_r.at[source],
            {"seq": source},
        )
    for index in range(n):
        arrival(
            next_hbm.at[0, :, cols_of(index)], blk_s.at[index], blk_r.at[index],
            {"section": before, "seq": index},
        )
    for copy in sends:
        copy.wait_send()


def fused(hidden, kv_cache, w_qkv, w_out, norm_gain, modulation, patch_order, timestep):
    n = lax.axis_size("seq")
    sections = lax.axis_size("section")
    tokens, width = hidden.shape[1:]
    patches = kv_cache.shape[1]
    cols = w_qkv.shape[3]
    rows = n * tokens
    chunk = width // 3 if width % 48 == 0 else width
    parts = width // chunk
    wide = cols * 2 // 3 // 256 * 256
    if wide % norm_gain.shape[2]:
        wide = 0
    cuts = ((0, wide), (wide, cols)) if wide else ((0, cols),)
    bf16, f32 = jnp.bfloat16, jnp.float32
    anywhere = pl.BlockSpec(memory_space=pl.ANY)
    in_hbm = pl.BlockSpec(memory_space=pltpu.HBM)
    dma = pltpu.SemaphoreType.DMA
    return pl.pallas_call(
        functools.partial(fused_kernel, n, sections, chunk, cuts),
        out_shape=(
            pltpu.VMEM(hidden.shape, bf16),
            pltpu.VMEM((1, tokens, 2, width), bf16),
        ),
        in_specs=[in_hbm] * 8,
        out_specs=(anywhere, anywhere),
        scratch_shapes=[
            pltpu.VMEM((tokens, width), bf16),
            pltpu.VMEM((n, tokens, cols), bf16),
            pltpu.VMEM((n, tokens, width), bf16),
            pltpu.VMEM((rows, width), f32),
            pltpu.VMEM((patches, tokens, 2, width), bf16),
            pltpu.VMEM((2, n, patches - 1, tokens, cols), bf16),
            pltpu.VMEM((2, n, patches - 1, tokens, cols), bf16),
            pltpu.VMEM((2, patches * rows, cols), f32),
            pltpu.VMEM((3, width, cols), bf16),
            pltpu.VMEM((n, cols, cols), bf16),
            pltpu.VMEM(norm_gain.shape, f32),
            pltpu.VMEM((3, modulation.shape[1], width), f32),
            pltpu.SMEM(patch_order.shape, jnp.int32),
            pltpu.SMEM(timestep.shape, jnp.int32),
            pltpu.VMEM((n, tokens, 2, cols), bf16),
            pltpu.VMEM((n, rows, cols), bf16),
            pltpu.VMEM((n, tokens, cols), bf16),
            dma((3, parts)),
            dma((n,)),
            dma((7,)),
            dma((parts, n)),
            dma((parts, n)),
        ]
        + [dma((n,))] * 8
        + [dma((len(cuts), n))] * 2
        + [dma((n,))] * 2,
        compiler_params=pltpu.CompilerParams(
            collective_id=0, has_side_effects=True, vmem_limit_bytes=60 * 2**20
        ),
    )(
        patch_order,
        timestep,
        hidden,
        kv_cache,
        jnp.transpose(w_qkv[0], (1, 0, 2)),
        w_out[0].reshape(n, cols, cols),
        norm_gain,
        jnp.transpose(modulation[0], (1, 0, 2)),
    )


def block_step(*arrays):
    hidden, w_qkv, norm_gain = arrays[0], arrays[2], arrays[4]
    lanes = norm_gain.shape[2]
    whole_heads = lanes % 128 == 0 and w_qkv.shape[3] % lanes == 0
    whole_tiles = lax.axis_size("seq") * hidden.shape[1] % 16 == 0 and arrays[1].shape[1] > 1
    if whole_heads and whole_tiles and lax.axis_size("seq") > 1 and lax.axis_size("section") > 1:
        return fused(*arrays)
    return body(*arrays)


def solution(mesh):
    return jax.shard_map(
        block_step,
        mesh=mesh,
        in_specs=(
            P("section", ("groups", "seq"), None),
            P("section", None, ("groups", "seq"), None, None),
            P("section", None, None, "seq"),
            P("section", None, "seq"),
            P("section", None, None),
            P("section", None, None, None),
            P("groups"),
            P("groups"),
        ),
        out_specs=(
            P("section", ("groups", "seq"), None),
            P("section", ("groups", "seq"), None, None),
        ),
        check_vma=False,
    )
```

```python
import functools
import math

import jax
import jax.numpy as jnp
from jax import lax
from jax.experimental import pallas as pl
from jax.experimental.pallas import tpu as pltpu
from jax.sharding import PartitionSpec as P


def passed_along(array, axis, by):
    count = lax.axis_size(axis)
    return lax.ppermute(array, axis, [(i, (i + by) % count) for i in range(count)])


def layer_norm(values_in):
    center = values_in - jnp.mean(values_in, axis=-1, keepdims=True)
    spread = jnp.mean(center * center, axis=-1, keepdims=True)
    return center * lax.rsqrt(spread + 1e-06)


def head_norm(values_in, gain):
    square = jnp.mean(values_in * values_in, axis=-1, keepdims=True)
    return values_in * lax.rsqrt(square + 1e-06) * gain


def body(hidden, kv_cache, w_qkv, w_out, norm_gain, modulation, patch_order, timestep):
    section_index = lax.axis_index("section")
    patch_index = lax.dynamic_index_in_dim(patch_order, section_index, 0, keepdims=False)
    step_index = lax.dynamic_index_in_dim(timestep, section_index, 0, keepdims=False)
    modulate = lax.dynamic_index_in_dim(modulation[0], step_index, 0, keepdims=False)
    model_width = hidden.shape[2]
    head_size = norm_gain.shape[2]
    head_count = model_width // head_size
    col_width = w_qkv.shape[3]
    rows_in = hidden[0].astype(jnp.float32)
    own_count = rows_in.shape[0]
    normed = (layer_norm(rows_in) * (1.0 + modulate[1]) + modulate[0]).astype(jnp.bfloat16)
    w_local = w_qkv[0].reshape(model_width, 3 * col_width)
    projected = jnp.dot(
        lax.all_gather(normed, "seq", axis=0, tiled=True),
        w_local,
        preferred_element_type=jnp.float32,
    ).astype(jnp.bfloat16)
    patch_len = projected.shape[0]
    projected = projected.reshape(patch_len, 3, col_width)
    query_cols = lax.all_gather(projected[:, 0], "seq", axis=1, tiled=True)
    kv_rows = lax.all_to_all(projected[:, 1:], "seq", split_axis=0, concat_axis=2, tiled=True)
    queries = head_norm(
        query_cols.astype(jnp.float32).reshape(patch_len, head_count, head_size), norm_gain[0, 0]
    ).astype(jnp.bfloat16)
    key_rows = head_norm(
        kv_rows[:, 0].astype(jnp.float32).reshape(own_count, head_count, head_size), norm_gain[0, 1]
    ).astype(jnp.bfloat16)
    fresh = jnp.stack([key_rows.reshape(own_count, model_width), kv_rows[:, 1]], axis=1)
    zero = jnp.zeros((), jnp.int32)
    local_kv = lax.dynamic_update_slice(kv_cache[0], fresh[None], (patch_index, zero, zero, zero))
    patch_count = local_kv.shape[0]
    local_keys = local_kv[:, :, 0].reshape(patch_count * own_count, head_count, head_size)
    local_values = local_kv[:, :, 1].reshape(patch_count * own_count, head_count, head_size)
    scores = jnp.einsum(
        "thd,shd->hts", queries, local_keys, preferred_element_type=jnp.float32
    ) / math.sqrt(head_size)
    row_top = lax.pmax(jnp.max(scores, axis=-1), "seq")
    weights = jnp.exp(scores - row_top[:, :, None]).astype(jnp.bfloat16)
    denominator = jnp.sum(weights, axis=-1, dtype=jnp.float32).T
    numerator = jnp.einsum(
        "hts,shd->thd", weights, local_values, preferred_element_type=jnp.float32
    ).reshape(patch_len, model_width)
    totals, counts = (
        lax.psum(numerator.astype(jnp.bfloat16), "seq").astype(jnp.float32),
        lax.psum(denominator.astype(jnp.bfloat16), "seq").astype(jnp.float32),
    )
    attention = (totals.reshape(patch_len, head_count, head_size) / counts[:, :, None]).astype(
        jnp.bfloat16
    )
    attention = attention.reshape(patch_len, model_width)
    out_cols = jnp.dot(attention, w_out[0], preferred_element_type=jnp.float32).astype(jnp.bfloat16)
    out_rows = lax.all_to_all(out_cols, "seq", split_axis=0, concat_axis=1, tiled=True)
    block = (rows_in + modulate[2] * out_rows.astype(jnp.float32)).astype(jnp.bfloat16)
    arrived = passed_along(block, "section", 1)
    return (arrived[None], fresh[None])


MESH = pl.DeviceIdType.MESH


def fused_kernel(
    n, sections, chunk, cuts,
    patch_hbm, step_hbm, hidden_hbm, cache_hbm, qkv_hbm, out_hbm, gain_hbm, mod_hbm,
    next_ref, fresh_hbm,
    own_rows, prev_rows, gate_row, prev_gate, landed, norm_buf, rows_f32, own_cache, cache_stage, cache_in, all_f32, w_qkv, w_out,
    gain, mod, patch, step_at, fresh_stage, att_buf, block_stage,
    sem_qkv, sem_out, sem_small, norm_s, norm_r, hid_sems, key_s, key_r, value_s, value_r,
    fresh_s, fresh_r, att_s, att_r, blk_s, blk_r,
):
    f32, bf16 = jnp.float32, jnp.bfloat16
    me = lax.axis_index("seq")
    section = lax.axis_index("section")
    after = lax.rem(section + 1, sections)
    before = lax.rem(section + sections - 1, sections)
    tokens, width = own_rows.shape
    cols = w_qkv.shape[2]
    patches = own_cache.shape[0]
    head = gain.shape[2]
    heads = cols // head
    rows = n * tokens
    kept = patches - 1
    per = kept * tokens
    stale = n * per
    parts = width // chunk

    def cols_of(index):
        return pl.ds(pl.multiple_of(index * cols, head), cols)

    upper = me >= n // 2
    edge = jnp.where(upper, n - 1 - me, me)

    def origin(step):
        index = step - 1 + jnp.where(edge <= step - 1, 1, 0)
        return jnp.where(upper, n - 1 - index, index)

    def peer(step):
        return origin(n - step)

    barrier = pltpu.get_barrier_semaphore()
    for step in range(1, n):
        pl.semaphore_signal(
            barrier, inc=1, device_id={"seq": peer(step)}, device_id_type=MESH
        )
    for index in range(n):
        pl.semaphore_signal(
            barrier, inc=1, device_id={"section": before, "seq": index}, device_id_type=MESH
        )
    small = [
        pltpu.make_async_copy(src, dst, sem_small.at[place])
        for place, (src, dst) in enumerate(
            (
                (hidden_hbm.at[0], own_rows),
                (mod_hbm, mod),
                (step_hbm, step_at),
                (patch_hbm, patch),
                (gain_hbm, gain),
                (cache_hbm.at[0], own_cache),
            )
        )
    ]
    for copy in small:
        copy.start()
    qkv_copies = {}
    for part in range(parts):
        for which in (1, 0, 2):
            span = pl.ds(part * chunk, chunk)
            copy = pltpu.make_async_copy(
                qkv_hbm.at[which, span], w_qkv.at[which, span], sem_qkv.at[which, part]
            )
            qkv_copies[which, part] = copy
            if part == 0:
                copy.start()

    for copy in small[:3]:
        copy.wait()
    chosen = lax.broadcasted_iota(jnp.int32, (mod.shape[1], 1), 0) == step_at[section]
    shift, scale = (
        jnp.sum(jnp.where(chosen, mod[which], 0.0), axis=0, keepdims=True) for which in range(2)
    )
    rows_in = own_rows[...].astype(f32)
    center = rows_in - jnp.mean(rows_in, axis=-1, keepdims=True)
    spread = jnp.mean(center * center, axis=-1, keepdims=True)
    norm_buf[me] = (center * lax.rsqrt(spread + 1e-06) * (1.0 + scale) + shift).astype(bf16)
    pl.semaphore_wait(barrier, 2 * n - 1)

    sends = []

    def send(src, dst, send_sem, recv_sem, device):
        copy = pltpu.make_async_remote_copy(
            src_ref=src, dst_ref=dst, send_sem=send_sem, recv_sem=recv_sem,
            device_id=device, device_id_type=MESH,
        )
        copy.start()
        sends.append(copy)

    def arrival(dst, send_sem, recv_sem, device):
        pltpu.make_async_remote_copy(
            src_ref=dst, dst_ref=dst, send_sem=send_sem, recv_sem=recv_sem,
            device_id=device, device_id_type=MESH,
        ).wait_recv()

    for part in range(parts):
        piece = norm_buf.at[me, :, pl.ds(part * chunk, chunk)]
        for step in range(1, n):
            send(piece, piece, norm_s.at[part, step], norm_r.at[part, me], {"seq": peer(step)})

    for (which, part), copy in qkv_copies.items():
        if part > 0:
            copy.start()

    for copy in small[3:]:
        copy.wait()
    held = patch[section]
    for slot in range(kept):
        pair = jnp.where(held <= slot, own_cache[slot + 1], own_cache[slot]).astype(f32)
        for which in range(2):
            split = pair[:, which, :].astype(bf16)
            for index in range(n):
                cache_stage[which, index, slot] = split[:, index * cols : (index + 1) * cols]
    for which, (send_sem, recv_sem) in enumerate(((key_s, key_r), (value_s, value_r))):
        for step in range(1, n):
            send(
                cache_stage.at[which, peer(step)], cache_in.at[which, me],
                send_sem.at[step], recv_sem.at[me], {"seq": peer(step)},
            )
        cache_in[which, me] = cache_stage[which, me]
    gate_row[...] = jnp.sum(jnp.where(chosen, mod[2], 0.0), axis=0, keepdims=True)
    send(own_rows, prev_rows, hid_sems.at[0], hid_sems.at[1], {"section": after})
    send(gate_row, prev_gate, hid_sems.at[2], hid_sems.at[3], {"section": after})
    out_copies = [
        pltpu.make_async_copy(out_hbm.at[index], w_out.at[index], sem_out.at[index])
        for index in range(n)
    ]
    for copy in out_copies:
        copy.start()

    totals = [jnp.zeros((rows, cuts[0][1]), f32)] * 3
    for part in range(parts):
        span = slice(part * chunk, (part + 1) * chunk)
        for step in range(1, n):
            source = origin(step)
            arrival(
                norm_buf.at[source, :, pl.ds(part * chunk, chunk)],
                norm_s.at[part, step], norm_r.at[part, source], {"seq": source},
            )
        for index in range(n):
            rows_f32[index * tokens : (index + 1) * tokens, span] = norm_buf[index, :, span].astype(
                f32
            )
        normed = rows_f32[:, span].astype(bf16)
        for which in (1, 0, 2):
            qkv_copies[which, part].wait()
            totals[which] += jnp.dot(
                normed, w_qkv[which, span, : cuts[0][1]], preferred_element_type=f32
            )
    normed = rows_f32[...].astype(bf16)
    projected = [[total.astype(bf16) for total in totals]]

    def arrivals(which, send_sem, recv_sem):
        for step in range(1, n):
            source = origin(step)
            arrival(
                cache_in.at[which, source], send_sem.at[step], recv_sem.at[source], {"seq": source}
            )
        for index in range(n):
            for slot in range(kept):
                first = index * per + slot * tokens
                all_f32[which, first : first + tokens, :] = cache_in[which, index, slot].astype(f32)

    def head_norms(projected, which):
        done = []
        for index in range(projected.shape[1] // head):
            vector = projected[:, index * head : (index + 1) * head].astype(f32)
            square = jnp.mean(vector * vector, axis=-1, keepdims=True)
            normal = vector * lax.rsqrt(square + 1e-06) * gain[0, which : which + 1, :]
            done.append(normal.astype(bf16))
        return done

    count = stale + rows
    column = lax.broadcasted_iota(jnp.int32, (1, count), 1)
    group = jnp.where(column < stale, column // per, (column - stale) // tokens)
    row_group = lax.broadcasted_iota(jnp.int32, (n * rows, 1), 0) // rows
    same_group = row_group == group
    ones = jnp.ones((count, head), bf16)

    def prepare(projected, first):
        fresh = jnp.concatenate(head_norms(projected[1], 1), axis=1)
        span = slice(first, first + fresh.shape[1])
        all_f32[0, stale:, span] = fresh.astype(f32)
        all_f32[1, stale:, span] = projected[2].astype(f32)
        return head_norms(projected[0], 0)

    def weigh(queries, first):
        weights = []
        for index, query in enumerate(queries):
            span = slice(first + index * head, first + (index + 1) * head)
            scores = lax.dot_general(
                query, all_f32[0, :, span].astype(bf16),
                (((1,), (1,)), ((), ())), preferred_element_type=f32,
            ) * (1.0 / math.sqrt(head))
            top = jnp.max(scores, axis=-1, keepdims=True)
            weight = jnp.exp(scores - top)
            grouped = jnp.where(same_group, jnp.concatenate([weight] * n, axis=0), 0.0)
            weights.append(grouped.astype(bf16))
        return weights

    arrivals(0, key_s, key_r)
    for first, last in cuts[1:]:
        projected.append(
            [
                jnp.dot(normed, w_qkv[which, :, first:last], preferred_element_type=f32).astype(bf16)
                for which in range(3)
            ]
        )
    queries = [prepare(part, first) for (first, _), part in zip(cuts, projected)]
    weights = weigh(queries[0], 0)

    is_key = lax.broadcasted_iota(jnp.int32, (tokens, 2, cols), 1) == 0
    for index in range(n):
        span = slice(stale + index * tokens, stale + (index + 1) * tokens)
        fresh_stage[index] = jnp.where(
            is_key, all_f32[0, span, :][:, None, :], all_f32[1, span, :][:, None, :]
        ).astype(bf16)
    arrivals(1, value_s, value_r)
    for place, (first, last) in enumerate(cuts):
        if place > 0:
            weights += weigh(queries[place], first)
        for index in range(first // head, last // head):
            span = slice(index * head, (index + 1) * head)
            both = jnp.concatenate([all_f32[1, :, span].astype(bf16), ones], axis=1)
            partial = jnp.dot(weights[index], both, preferred_element_type=f32)
            partial = partial.astype(bf16).astype(f32)
            sums = sum(partial[i * rows : (i + 1) * rows] for i in range(n))
            att_buf[me, :, span] = (sums[:, :head] / sums[:, head:]).astype(bf16)
        piece = att_buf.at[me, :, pl.ds(first, last - first)]
        for step in range(1, n):
            send(piece, piece, att_s.at[place, step], att_r.at[place, me], {"seq": peer(step)})

    for copy in out_copies:
        copy.wait()
    total = jnp.dot(att_buf[me], w_out[me], preferred_element_type=f32)
    for place, (first, last) in enumerate(cuts):
        for step in range(1, n):
            source = origin(step)
            arrival(
                att_buf.at[source, :, pl.ds(first, last - first)],
                att_s.at[place, step], att_r.at[place, source], {"seq": source},
            )
            if place == len(cuts) - 1 and step == n - 1:
                own_fresh = pltpu.make_async_copy(
                    fresh_stage.at[me], fresh_hbm.at[0, :, :, cols_of(me)], sem_small.at[6]
                )
                own_fresh.start()
                for other in range(1, n):
                    send(
                        fresh_stage.at[peer(other)], fresh_hbm.at[0, :, :, cols_of(me)],
                        fresh_s.at[other], fresh_r.at[me], {"seq": peer(other)},
                    )
            total += jnp.dot(
                att_buf[source, :, first:last], w_out[source, first:last, :],
                preferred_element_type=f32,
            )
    for index in range(n):
        block_stage[index] = total[index * tokens : (index + 1) * tokens].astype(bf16)
    for index in range(n):
        send(
            block_stage.at[index], landed.at[me], blk_s.at[index], blk_r.at[me],
            {"section": after, "seq": index},
        )
    arrival(prev_rows, hid_sems.at[0], hid_sems.at[1], {"section": before})
    arrival(prev_gate, hid_sems.at[2], hid_sems.at[3], {"section": before})
    own_fresh.wait()
    for step in range(1, n):
        source = origin(step)
        arrival(
            fresh_hbm.at[0, :, :, cols_of(source)], fresh_s.at[step], fresh_r.at[source],
            {"seq": source},
        )
    for index in range(n):
        arrival(landed.at[index], blk_s.at[index], blk_r.at[index], {"section": before, "seq": index})
        span = slice(index * cols, (index + 1) * cols)
        change = prev_gate[:, span] * landed[index].astype(f32)
        next_ref[0, :, span] = (prev_rows[:, span].astype(f32) + change).astype(bf16)
    for copy in sends:
        copy.wait_send()


def fused(hidden, kv_cache, w_qkv, w_out, norm_gain, modulation, patch_order, timestep):
    n = lax.axis_size("seq")
    sections = lax.axis_size("section")
    tokens, width = hidden.shape[1:]
    patches = kv_cache.shape[1]
    cols = w_qkv.shape[3]
    rows = n * tokens
    chunk = width // 3 if width % 48 == 0 else width
    parts = width // chunk
    wide = cols * 2 // 3 // 256 * 256
    if wide % norm_gain.shape[2]:
        wide = 0
    cuts = ((0, wide), (wide, cols)) if wide else ((0, cols),)
    bf16, f32 = jnp.bfloat16, jnp.float32
    anywhere = pl.BlockSpec(memory_space=pl.ANY)
    in_hbm = pl.BlockSpec(memory_space=pltpu.HBM)
    dma = pltpu.SemaphoreType.DMA
    return pl.pallas_call(
        functools.partial(fused_kernel, n, sections, chunk, cuts),
        out_shape=(
            pltpu.VMEM(hidden.shape, bf16),
            pltpu.VMEM((1, tokens, 2, width), bf16),
        ),
        in_specs=[in_hbm] * 8,
        out_specs=(pl.BlockSpec(memory_space=pltpu.VMEM), anywhere),
        scratch_shapes=[
            pltpu.VMEM((tokens, width), bf16),
            pltpu.VMEM((tokens, width), bf16),
            pltpu.VMEM((1, width), f32),
            pltpu.VMEM((1, width), f32),
            pltpu.VMEM((n, tokens, cols), bf16),
            pltpu.VMEM((n, tokens, width), bf16),
            pltpu.VMEM((rows, width), f32),
            pltpu.VMEM((patches, tokens, 2, width), bf16),
            pltpu.VMEM((2, n, patches - 1, tokens, cols), bf16),
            pltpu.VMEM((2, n, patches - 1, tokens, cols), bf16),
            pltpu.VMEM((2, patches * rows, cols), f32),
            pltpu.VMEM((3, width, cols), bf16),
            pltpu.VMEM((n, cols, cols), bf16),
            pltpu.VMEM(norm_gain.shape, f32),
            pltpu.VMEM((3, modulation.shape[1], width), f32),
            pltpu.SMEM(patch_order.shape, jnp.int32),
            pltpu.SMEM(timestep.shape, jnp.int32),
            pltpu.VMEM((n, tokens, 2, cols), bf16),
            pltpu.VMEM((n, rows, cols), bf16),
            pltpu.VMEM((n, tokens, cols), bf16),
            dma((3, parts)),
            dma((n,)),
            dma((7,)),
            dma((parts, n)),
            dma((parts, n)),
        ]
        + [dma((4,))]
        + [dma((n,))] * 6
        + [dma((len(cuts), n))] * 2
        + [dma((n,))] * 2,
        compiler_params=pltpu.CompilerParams(
            collective_id=0, has_side_effects=True, vmem_limit_bytes=60 * 2**20
        ),
    )(
        patch_order,
        timestep,
        hidden,
        kv_cache,
        jnp.transpose(w_qkv[0], (1, 0, 2)),
        w_out[0].reshape(n, cols, cols),
        norm_gain,
        jnp.transpose(modulation[0], (1, 0, 2)),
    )


def block_step(*arrays):
    hidden, w_qkv, norm_gain = arrays[0], arrays[2], arrays[4]
    lanes = norm_gain.shape[2]
    whole_heads = lanes % 128 == 0 and w_qkv.shape[3] % lanes == 0
    whole_tiles = lax.axis_size("seq") * hidden.shape[1] % 16 == 0 and arrays[1].shape[1] > 1
    if whole_heads and whole_tiles and lax.axis_size("seq") > 1 and lax.axis_size("section") > 1:
        return fused(*arrays)
    return body(*arrays)


def solution(mesh):
    return jax.shard_map(
        block_step,
        mesh=mesh,
        in_specs=(
            P("section", ("groups", "seq"), None),
            P("section", None, ("groups", "seq"), None, None),
            P("section", None, None, "seq"),
            P("section", None, "seq"),
            P("section", None, None),
            P("section", None, None, None),
            P("groups"),
            P("groups"),
        ),
        out_specs=(
            P("section", ("groups", "seq"), None),
            P("section", ("groups", "seq"), None, None),
        ),
        check_vma=False,
    )
```
